128 devices in a mesh: tm: 32 (over z, y, core), head: 4 (over x).
Axes of the slice: x: 4, y: 4, z: 4, core: 2. Of those that a mesh axis runs over, the one named last changes fastest.
Arguments:
- tokens: bfloat16 [100352, 1024], P('tm'), may hold values from -11 to 11
- w_query: bfloat16 [1024, 1024], P(None, 'head'), may hold values from -1 to 1
- w_key: bfloat16 [1024, 1024], P(None, 'head'), may hold values from -1 to 1
- w_value: bfloat16 [1024, 1024], P(None, 'head'), may hold values from -0.1875 to 0.1875
- w_out: bfloat16 [1024, 1024], P('head'), may hold values from -3 to 3
- pattern: int32 [512, 512], P('tm'), may hold values 0 or 1
- visible: int32 [512, 20], P('tm'), may hold values from 0 to 195, as said below
- slot: int32 [10240], replicated, may hold values from 0 to 10239, as said below
- pred: bfloat16 [10240, 1024], P('tm', 'head'), may hold values from -6 to 6
Outputs:
- target: bfloat16 [10240, 1024], P('tm', 'head')
- row_loss: float32 [10240], P('tm')
The draws below stay inside these ranges and needn't reach their ends.
Inputs may be any that keep to these rules, and one draw needn't show every extreme that they name: `visible`: each row holds 20 different positions in rising order; frames 2 t and 2 t + 1 have the same row. `slot`: A permutation of the visible rows. Of the 320 visible rows of one tm index, at most 41 have student rows of any one tm index (student rows 320 o to 320 o + 319 belong to tm index o), exactly 41 for one of them and at least 9 for every one.
All inputs are finite; a program needn't handle non-finite values. No bound on the sum of `pattern` on one device may be relied on, other than what follows from the above.
Results may differ from the reference program's by a relative error of at most 0.0085.
Values may be sent and summed in bfloat16 or wider, within the bound.
No kernel may reach another device: no remote copies, remote signals or barrier semaphores. Data moves between devices by JAX's collectives and lax.ppermute only.
A program may use at most 128 MiB of HBM per device.

```python
import math
import jax
import jax.numpy as jnp
from jax import lax

D = 1024
HEADS = 16
HEAD_DIM = 64
PATCHES = 196
KEEP = 20
FRAMES = 512
ROWS_DEV = 320
VIS = 10240


def shared_weight(weight_key):
    return jnp.clip(jax.random.normal(weight_key, (D, D), jnp.float32), -4.0, 4.0) / math.sqrt(D)


def draw_w_query(key, part):
    common = shared_weight(key)
    return common.astype(jnp.bfloat16)


def draw_w_key(key, part):
    key = jax.random.fold_in(key, 13)
    own_part = shared_weight(key)
    return own_part.astype(jnp.bfloat16)


def draw_tokens(key, part):
    key = jax.random.fold_in(key, 3)
    first_key = jax.random.fold_in(key, 0)
    values = jnp.clip(jax.random.normal(first_key, (FRAMES * PATCHES, D), jnp.float32), -4.0, 4.0)
    return values.astype(jnp.bfloat16)


def draw_visible(key, part):
    key = jax.random.fold_in(key, 5)
    tube_keys = jax.random.split(key, FRAMES // 2)
    chosen = jax.vmap(lambda tube_key: jnp.sort(jax.random.permutation(tube_key, PATCHES)[:KEEP]))(tube_keys)
    return jnp.repeat(chosen, 2, axis=0).astype(jnp.int32)


def draw_slot(key, part):
    key = jax.random.fold_in(key, 7)
    first_key, second_key, third_key = jax.random.split(key, 3)
    n_peers = VIS // ROWS_DEV
    floor_share = ROWS_DEV // (n_peers + 3)
    heavy_share = ROWS_DEV - n_peers * floor_share
    partner = jax.random.permutation(first_key, n_peers).astype(jnp.int32)
    position = jnp.arange(ROWS_DEV, dtype=jnp.int32)
    spread_dest = jnp.clip((position - heavy_share) // floor_share, 0, n_peers - 1)
    dest_table = jnp.where(position[None, :] < heavy_share, partner[:, None], spread_dest[None, :])
    shuffles = jax.vmap(lambda row_key: jax.random.permutation(row_key, ROWS_DEV))(jax.random.split(second_key, n_peers))
    dest_table = jnp.take_along_axis(dest_table, shuffles.astype(jnp.int32), axis=1).reshape(-1)
    tie_break = jax.random.permutation(third_key, VIS).astype(jnp.int32)
    ordering = jnp.argsort(dest_table * VIS + tie_break)
    return jnp.zeros((VIS,), jnp.int32).at[ordering].set(jnp.arange(VIS, dtype=jnp.int32))


def place_ends(array, stream_key, least, largest):
    place = [jax.random.randint(jax.random.fold_in(stream_key, axis), (), 0, length) for axis, length in enumerate(array.shape)]
    main_axis = array.shape.index(max(array.shape))
    next_to = place[:main_axis] + [(place[main_axis] + 1) % array.shape[main_axis]] + place[main_axis + 1:]
    return array.at[tuple(place)].set(least).at[tuple(next_to)].set(largest)


def shard_levels(own_key, shape, cuts, least, largest):
    def one(axis_at, blocks):
        heights = jax.random.uniform(jax.random.fold_in(jax.random.fold_in(own_key, 6), axis_at), (blocks,), jnp.float32, least / len(cuts), largest / len(cuts))
        return jnp.repeat(jnp.exp(heights), shape[axis_at] // blocks).reshape((-1,) + (1,) * (len(shape) - axis_at - 1))

    loudness = one(*cuts[0])
    for cut in cuts[1:]:
        loudness = loudness * one(*cut)
    return loudness


def centred(key, dims, scale, limit, cuts=(), kind=jnp.bfloat16):
    loudness = shard_levels(key, dims, cuts, -0.22, 0.18) if cuts else 1.0
    values = jax.random.normal(key, dims, jnp.float32) * scale * loudness
    return jnp.minimum(jnp.maximum(values, -limit), limit).astype(kind)


def setup_inputs(seed: int = 0) -> dict:
    streams_of = jax.random.split(jax.random.key(seed), 10)
    return {
        "tokens": draw_tokens(jax.random.fold_in(streams_of[9], 71), 0),
        "w_query": draw_w_query(jax.random.fold_in(streams_of[9], 71), 0),
        "w_key": draw_w_key(jax.random.fold_in(streams_of[9], 71), 0),
        "w_value": centred(streams_of[3], (D, D), D ** -0.5, 0.1875, ((1, 4),)),
        "w_out": centred(streams_of[4], (D, D), 0.5, 3.0, ((0, 4),)),
        "pattern": place_ends((jax.random.randint(streams_of[5], (FRAMES, FRAMES), 0, 4) < 1).astype(jnp.int32), jax.random.fold_in(streams_of[5], 1), 0, 1),
        "visible": draw_visible(jax.random.fold_in(streams_of[9], 71), 0),
        "slot": draw_slot(jax.random.fold_in(streams_of[9], 71), 0),
        "pred": centred(streams_of[8], (VIS, D), 1.0, 6.0, ((0, 32), (1, 4))),
    }


epsilon = 1e-06

def pool_quadrants(field_rows, frame_count, model_width):
    tile_grid = field_rows.reshape(frame_count, 2, 7, 2, 7, model_width).astype(jnp.float32)
    pooled = lax.optimization_barrier(jnp.sum(tile_grid, axis=(2, 4))) / 7.0
    return pooled.reshape(frame_count * 4, model_width).astype(jnp.bfloat16)

def reference(tokens, w_query, w_key, w_value, w_out, pattern, visible, slot, pred):
    frame_count = visible.shape[0]
    model_width = tokens.shape[1]
    queries = jnp.dot(tokens, w_query, preferred_element_type=jnp.float32).astype(jnp.bfloat16)
    keys_all = jnp.dot(tokens, w_key, preferred_element_type=jnp.float32).astype(jnp.bfloat16)
    values_all = jnp.dot(tokens, w_value, preferred_element_type=jnp.float32).astype(jnp.bfloat16)
    summary_keys = pool_quadrants(keys_all, frame_count, model_width).reshape(frame_count * 4, HEADS, HEAD_DIM).astype(jnp.float32)
    summary_values = pool_quadrants(values_all, frame_count, model_width).reshape(frame_count * 4, HEADS, HEAD_DIM).astype(jnp.float32)
    allowed = jnp.repeat(pattern, 4, axis=1)
    score_scale = HEAD_DIM ** (-0.5)
    frame_shape = (frame_count, PATCHES, HEADS, HEAD_DIM)

    def one_frame(inputs):
        frame_q, frame_k, frame_v, allow_row = inputs
        frame_q = frame_q.astype(jnp.float32)
        local_scores = jnp.einsum('qhd,khd->hqk', frame_q, frame_k.astype(jnp.float32)) * score_scale
        far_scores = jnp.einsum('qhd,shd->hqs', frame_q, summary_keys) * score_scale
        far_scores = jnp.where(allow_row[None, None, :] > 0, far_scores, -jnp.inf)
        row_top = jnp.maximum(lax.optimization_barrier(jnp.max(local_scores, axis=2)), lax.optimization_barrier(jnp.max(far_scores, axis=2)))[:, :, None]
        local_exp = jnp.exp(local_scores - row_top)
        far_exp = jnp.exp(far_scores - row_top)
        row_total = lax.optimization_barrier(jnp.sum(local_exp, axis=2, keepdims=True)) + lax.optimization_barrier(jnp.sum(far_exp, axis=2, keepdims=True))
        local_weights = (local_exp / row_total).astype(jnp.bfloat16).astype(jnp.float32)
        far_weights = (far_exp / row_total).astype(jnp.bfloat16).astype(jnp.float32)
        mixed_out = jnp.einsum('hqk,khd->qhd', local_weights, frame_v.astype(jnp.float32))
        mixed_out = mixed_out + jnp.einsum('hqs,shd->qhd', far_weights, summary_values)
        return mixed_out.astype(jnp.bfloat16)
    attended = lax.map(one_frame, (queries.reshape(frame_shape), keys_all.reshape(frame_shape), values_all.reshape(frame_shape), allowed))
    attended = attended.reshape(frame_count * PATCHES, model_width)
    positions = (jnp.arange(frame_count, dtype=jnp.int32)[:, None] * PATCHES + visible).reshape(-1).astype(jnp.int32)
    raw_rows = tokens[positions].astype(jnp.float32) + jnp.dot(attended[positions], w_out, preferred_element_type=jnp.float32)
    placed = jnp.zeros_like(raw_rows).at[slot].set(raw_rows)
    row_mean = lax.optimization_barrier(jnp.sum(placed, axis=1)) / model_width
    row_var = lax.optimization_barrier(jnp.sum(placed * placed, axis=1)) / model_width - row_mean * row_mean
    normed = (placed - row_mean[:, None]) * lax.rsqrt(row_var + epsilon)[:, None]
    pred_rows = pred.astype(jnp.float32)
    row_loss = lax.optimization_barrier(jnp.sum((pred_rows - normed) ** 2, axis=1)) / model_width
    return (normed.astype(jnp.bfloat16), row_loss)
```

```python
import numpy as np

import jax
import jax.numpy as jnp
from jax import lax
from jax.experimental import pallas as pl
from jax.experimental.pallas import tpu as pltpu
from jax.sharding import PartitionSpec as P

HEAD_DIM = 64
PATCHES = 196
CAP = 48
NEG = -1e30
EPS = 1e-06
BF = jnp.bfloat16
F32 = jnp.float32


def nt(a, b):
    return lax.dot_general(a, b, (((1,), (1,)), ((), ())), preferred_element_type=F32)


def nn(a, b):
    return lax.dot_general(a, b, (((1,), (0,)), ((), ())), preferred_element_type=F32)


def project_kernel(x_ref, wq_ref, wk_ref, wv_ref, pool_ref, pos_ref, k_ref, v_ref, s_ref, q_ref, vis_ref):
    x = x_ref[...]
    rows = x.shape[0]
    keep = pos_ref.shape[0]
    cols = wk_ref.shape[1]
    k = nn(x, wk_ref[...]).astype(BF)
    v = nn(x, wv_ref[...]).astype(BF)
    k_ref[...] = k
    v_ref[...] = v
    pool = pool_ref[...]
    s_ref[:, :, :cols] = (nn(pool, k) / 7.0).astype(BF).reshape(4, 4, cols)
    s_ref[:, :, cols:] = (nn(pool, v) / 7.0).astype(BF).reshape(4, 4, cols)
    pick = (pos_ref[...] == lax.broadcasted_iota(jnp.int32, (keep, rows), 1)).astype(F32).astype(BF)
    vis = nn(pick, x).astype(BF)
    vis_ref[...] = vis
    q_ref[...] = (nn(vis, wq_ref[...]).astype(BF).astype(F32) * HEAD_DIM ** -0.5).astype(BF)


def local_kernel(q_ref, k_ref, v_ref, o_ref, ml_ref):
    q = q_ref[...]
    k = k_ref[...]
    v = v_ref[...]
    rows, cols = q.shape
    keep = rows // 4
    heads = cols // HEAD_DIM
    r = lax.broadcasted_iota(jnp.int32, (rows, 1), 0)
    frame = sum((r >= keep * i).astype(jnp.int32) for i in (1, 2, 3))
    c = lax.broadcasted_iota(jnp.int32, (rows, k.shape[0]), 1) - frame * PATCHES
    inside = (c >= 0) & (c < PATCHES)
    lane = lax.broadcasted_iota(jnp.int32, (rows, cols), 1)
    lane2 = lax.broadcasted_iota(jnp.int32, (rows, 128), 1)
    out = jnp.zeros((rows, cols), F32)
    ml = jnp.zeros((rows, 128), F32)
    for h in range(heads):
        mine = (lane >= h * HEAD_DIM) & (lane < (h + 1) * HEAD_DIM)
        qh = jnp.where(mine, q, jnp.zeros_like(q))
        s = jnp.where(inside, nt(qh, k), NEG)
        m = jnp.max(s, axis=1, keepdims=True)
        e = jnp.exp(s - m)
        total = jnp.sum(e, axis=1, keepdims=True)
        out = jnp.where(mine, nn(e.astype(BF), v), out)
        ml = jnp.where(lane2 == h, m, jnp.where(lane2 == heads + h, total, ml))
    o_ref[...] = out
    ml_ref[...] = ml


def far_kernel(q_ref, sa_ref, sb_ref, pa_ref, pb_ref, pick_ref, o_ref, ml_ref, out_ref):
    q = q_ref[...]
    rows, cols = q.shape
    heads = cols // HEAD_DIM
    lane = lax.broadcasted_iota(jnp.int32, (rows, cols), 1)
    pick = pick_ref[...]
    bias = [nn(pick, p[...]) for p in (pa_ref, pb_ref)]
    count = sa_ref.shape[0] * 16
    out = jnp.zeros((rows, cols), F32)
    for h in range(heads):
        mine = (lane >= h * HEAD_DIM) & (lane < (h + 1) * HEAD_DIM)
        qh = jnp.where(mine, q, jnp.zeros_like(q))
        scores = []
        top = ml_ref[:, h : h + 1]
        for part, ref in enumerate((sa_ref, sb_ref)):
            for u in range(4):
                key = ref[:, u, :, :cols].reshape(count, cols)
                s = nt(qh, key) + bias[part]
                top = jnp.maximum(top, jnp.max(s, axis=1, keepdims=True))
                scores.append(s)
        near = jnp.exp(ml_ref[:, h : h + 1] - top)
        total = near * ml_ref[:, heads + h : heads + h + 1]
        acc = near * o_ref[...]
        for part, ref in enumerate((sa_ref, sb_ref)):
            for u in range(4):
                e = jnp.exp(scores[part * 4 + u] - top)
                total = total + jnp.sum(e, axis=1, keepdims=True)
                acc = acc + nn(e.astype(BF), ref[:, u, :, cols:].reshape(count, cols))
        out = jnp.where(mine, acc / total, out)
    out_ref[...] = out.astype(BF)


def whole(n):
    return [pl.BlockSpec(memory_space=pltpu.VMEM) for _ in range(n)]


def params(mib):
    return pltpu.CompilerParams(vmem_limit_bytes=mib * 2**20)


def tm_index(z, y, c):
    return ((z % 4) * 4 + y % 4) * 2 + c


SAME_CORE = [[tm_index(z, y, c) for z in range(4) for y in range(4)] for c in range(2)]


def body(tokens, w_query, w_key, w_value, w_out, pattern, visible, slot, pred):
    n_peers = lax.axis_size("tm")
    me = lax.axis_index("tm")
    core = me % 2
    head = lax.axis_index("head")
    n_heads = lax.axis_size("head")
    frames, keep = visible.shape
    width = tokens.shape[1]
    cols = w_query.shape[1]
    own = frames * keep
    steps = frames // 4
    block = 4 * PATCHES
    chunk = 4 * keep

    r = np.arange(block)
    p = r % PATCHES
    quadrant = 2 * (p // 14 >= 7) + (p % 14 >= 7)
    pool = np.zeros((16, block), np.float32)
    pool[quadrant * 4 + r // PATCHES, r] = 1.0
    pos = (jnp.arange(frames, dtype=jnp.int32)[:, None] % 4 * PATCHES + visible).reshape(own, 1)

    fixed = lambda i: (0, 0)
    k, v, summary, q, vis = pl.pallas_call(
        project_kernel,
        grid=(steps,),
        in_specs=[
            pl.BlockSpec((block, width), lambda i: (i, 0)),
            pl.BlockSpec((width, cols), fixed),
            pl.BlockSpec((width, cols), fixed),
            pl.BlockSpec((width, cols), fixed),
            pl.BlockSpec((16, block), fixed),
            pl.BlockSpec((chunk, 1), lambda i: (i, 0)),
        ],
        out_specs=[
            pl.BlockSpec((block, cols), lambda i: (i, 0)),
            pl.BlockSpec((block, cols), lambda i: (i, 0)),
            pl.BlockSpec((4, None, 4, 2 * cols), lambda i: (0, i, 0, 0)),
            pl.BlockSpec((chunk, cols), lambda i: (i, 0)),
            pl.BlockSpec((chunk, width), lambda i: (i, 0)),
        ],
        out_shape=[
            jax.ShapeDtypeStruct((frames * PATCHES, cols), BF),
            jax.ShapeDtypeStruct((frames * PATCHES, cols), BF),
            jax.ShapeDtypeStruct((4, steps, 4, 2 * cols), BF),
            jax.ShapeDtypeStruct((own, cols), BF),
            jax.ShapeDtypeStruct((own, width), BF),
        ],
        compiler_params=params(40),
        cost_estimate=pl.CostEstimate(flops=4 * 10**9, bytes_accessed=10**7, transcendentals=0),
        name="project",
    )(tokens, w_query, w_key, w_value, jnp.asarray(pool, BF), pos)
    summary = summary.reshape(4, frames, 2 * cols)

    gathered = lax.all_to_all(
        jnp.broadcast_to(summary[None], (n_peers // 2,) + summary.shape),
        "tm", 0, 0, axis_index_groups=SAME_CORE, tiled=True,
    )
    gathered_b = lax.ppermute(gathered, "tm", [(t, t ^ 1) for t in range(n_peers)])

    owner_all = slot // own
    my_slots = lax.dynamic_slice_in_dim(slot, me * own, own)
    my_owner = my_slots // own
    before = np.tril(np.ones((own, own), np.float32), -1)
    same = (my_owner[:, None] == my_owner[None, :]) & (before > 0)
    place = my_owner * CAP + jnp.sum(same, axis=1, dtype=jnp.int32)
    pack = (jnp.arange(n_peers * CAP, dtype=jnp.int32)[:, None] == place[None, :]).astype(BF)
    coming = (owner_all == me).reshape(n_peers, own)
    rank = jnp.dot(coming.astype(BF), jnp.asarray(before.T, BF), preferred_element_type=F32).astype(jnp.int32)
    rank = jnp.where(coming, rank, -1)
    hit = rank[:, None, :] == jnp.arange(CAP, dtype=jnp.int32)[None, :, None]
    student = jnp.max(jnp.where(hit, (slot % own).reshape(n_peers, 1, own), -1), axis=2)
    unpack = (jnp.arange(own, dtype=jnp.int32)[:, None] == student.reshape(1, -1)).astype(BF)

    def route(x):
        packed = jnp.dot(pack, x, preferred_element_type=F32).astype(BF).reshape(n_peers, CAP, -1)
        got = lax.all_to_all(packed, "tm", 0, 0, tiled=True)
        return jnp.dot(unpack, got.reshape(n_peers * CAP, -1), preferred_element_type=F32).astype(BF)

    token_rows = route(lax.dynamic_slice_in_dim(vis, head * cols, cols, 1))

    o_near, ml = pl.pallas_call(
        local_kernel,
        grid=(steps,),
        in_specs=[
            pl.BlockSpec((chunk, cols), lambda i: (i, 0)),
            pl.BlockSpec((block, cols), lambda i: (i, 0)),
            pl.BlockSpec((block, cols), lambda i: (i, 0)),
        ],
        out_specs=[
            pl.BlockSpec((chunk, cols), lambda i: (i, 0)),
            pl.BlockSpec((chunk, 128), lambda i: (i, 0)),
        ],
        out_shape=[
            jax.ShapeDtypeStruct((own, cols), F32),
            jax.ShapeDtypeStruct((own, 128), F32),
        ],
        compiler_params=params(40),
        cost_estimate=pl.CostEstimate(flops=10**9, bytes_accessed=4 * 10**6, transcendentals=10**6),
        name="near",
    )(q, k, v)

    banned = jnp.where(pattern > 0, 0.0, NEG).astype(BF).reshape(frames, n_peers // 2, 2, frames)
    ban_a = lax.dynamic_index_in_dim(banned, core, 2, keepdims=False).reshape(frames, -1)
    ban_b = lax.dynamic_index_in_dim(banned, 1 - core, 2, keepdims=False).reshape(frames, -1)
    pick = jnp.asarray(np.arange(own)[:, None] // keep == np.arange(frames)[None, :], BF)
    attended = pl.pallas_call(
        far_kernel,
        in_specs=whole(8),
        out_specs=pl.BlockSpec(memory_space=pltpu.VMEM),
        out_shape=jax.ShapeDtypeStruct((own, cols), BF),
        compiler_params=params(48),
        cost_estimate=pl.CostEstimate(flops=3 * 10**9, bytes_accessed=3 * 10**6, transcendentals=3 * 10**6),
        name="far",
    )(q, gathered, gathered_b, ban_a, ban_b, pick, o_near, ml)

    rows = route(attended)
    partial = jnp.dot(rows, w_out, preferred_element_type=F32)

    def column_block(h):
        return lax.dynamic_slice_in_dim(partial, (h % n_heads) * cols, cols, 1)

    def to(d):
        return [(h, (h + d) % n_heads) for h in range(n_heads)]

    raw = token_rows.astype(F32) + column_block(head)
    for d in (1, 3, 2):
        raw = raw + lax.ppermute(column_block(head + d).astype(BF), "head", to(d)).astype(F32)
    guess = pred.astype(F32)
    stats = jnp.stack([
        jnp.sum(raw, axis=1),
        jnp.sum(raw * raw, axis=1),
        jnp.sum(guess * raw, axis=1),
        jnp.sum(guess, axis=1),
        jnp.sum(guess * guess, axis=1),
    ])
    total = stats
    for d in (1, 3, 2):
        total = total + lax.ppermute(stats, "head", to(d))
    mean = total[0] / width
    var = total[1] / width - mean * mean
    scale = lax.rsqrt(var + EPS)
    normed = (raw - mean[:, None]) * scale[:, None]
    cross = (total[2] - mean * total[3]) * scale
    square = (total[1] - 2.0 * mean * total[0] + width * mean * mean) * scale * scale
    row_loss = (total[4] - 2.0 * cross + square) / width
    return normed.astype(BF), row_loss


def solution(mesh):
    return jax.shard_map(
        body,
        mesh=mesh,
        in_specs=(
            P("tm", None),
            P(None, "head"),
            P(None, "head"),
            P(None, "head"),
            P("head", None),
            P("tm", None),
            P("tm", None),
            P(),
            P("tm", "head"),
        ),
        out_specs=(P("tm", "head"), P("tm")),
        check_vma=False,
    )
```

```python
import numpy as np

import jax
import jax.numpy as jnp
from jax import lax
from jax.experimental import pallas as pl
from jax.experimental.pallas import tpu as pltpu
from jax.sharding import PartitionSpec as P

HEAD_DIM = 64
PATCHES = 196
CAP = 48
NEG = -1e30
EPS = 1e-06
BF = jnp.bfloat16
F32 = jnp.float32


def nt(a, b):
    return lax.dot_general(a, b, (((1,), (1,)), ((), ())), preferred_element_type=F32)


def nn(a, b):
    return lax.dot_general(a, b, (((1,), (0,)), ((), ())), preferred_element_type=F32)


def gather_kernel(head_ref, x_ref, wq_ref, wk_ref, wv_ref, pool_ref, pos_ref, order_ref, pat_ref, chunk_ref, qt_ref, sums, rows_in):
    step = pl.program_id(0)
    rows = x_ref.shape[0]
    keep = pos_ref.shape[0]
    cols = wk_ref.shape[1]
    x = x_ref[...]
    pick = (pos_ref[...] == lax.broadcasted_iota(jnp.int32, (keep, rows), 1)).astype(F32).astype(BF)
    both = nn(jnp.concatenate([pool_ref[...], pick], axis=0), x)
    sums[pl.ds(pl.multiple_of(step * 16, 16), 16), :] = both[:16]
    rows_in[pl.ds(pl.multiple_of(step * keep, 16), keep), :] = both[16:].astype(BF)

    @pl.when(step == pl.num_programs(0) - 1)
    def _():
        total = sums[...]
        count = total.shape[0]
        high = total.astype(BF)
        low = (total - high.astype(F32)).astype(BF)
        pair = jnp.concatenate([high, low], axis=0)
        order = order_ref[...]
        for i, w_ref in enumerate((wk_ref, wv_ref)):
            field = nn(pair, w_ref[...])
            pooled = ((field[:count] + field[count:]) / 7.0).astype(BF)
            chunk_ref[:count, i * cols : (i + 1) * cols] = nn(order, pooled).astype(BF)
        chunk_ref[count:, :] = pat_ref[...].astype(F32).astype(BF)
        q = nn(rows_in[...], wq_ref[...]).astype(BF).astype(F32) * HEAD_DIM ** -0.5
        qt_ref[:, :cols] = q.astype(BF)
        qt_ref[:, cols:] = rows_in[:, pl.ds(pl.multiple_of(head_ref[0] * cols, 128), cols)]


def near_kernel(q_ref, x_ref, wk_ref, wv_ref, out_ref):
    x = x_ref[...]
    k = nn(x, wk_ref[...]).astype(BF)
    v = nn(x, wv_ref[...]).astype(BF)
    q = q_ref[...]
    rows, cols = q.shape
    keep = rows // 4
    heads = cols // HEAD_DIM
    lane = lax.broadcasted_iota(jnp.int32, (rows, cols), 1)
    mine = [(lane >= h * HEAD_DIM) & (lane < (h + 1) * HEAD_DIM) for h in range(heads)]
    stack = jnp.concatenate([jnp.where(mine[h], q, jnp.zeros_like(q)) for h in range(heads)], axis=0)
    r = lax.broadcasted_iota(jnp.int32, (rows, 1), 0)
    frame = sum((r >= keep * i).astype(jnp.int32) for i in (1, 2, 3))
    c = lax.broadcasted_iota(jnp.int32, (rows, k.shape[0]), 1) - frame * PATCHES
    wall = jnp.where((c >= 0) & (c < PATCHES), 0.0, NEG)
    s = nt(stack, k) + jnp.concatenate([wall] * heads, axis=0)
    m = jnp.max(s, axis=1, keepdims=True)
    e = jnp.exp(s - m)
    total = jnp.sum(e, axis=1, keepdims=True)
    o = nn(e.astype(BF), v) / total
    level = m + jnp.log(total)
    high = level.astype(BF).astype(F32)
    middle = (level - high).astype(BF).astype(F32)
    low = level - high - middle
    lane2 = lax.broadcasted_iota(jnp.int32, (rows, 128), 1)
    out = jnp.zeros((rows, cols), F32)
    side = jnp.zeros((rows, 128), F32)
    for h in range(heads):
        part = slice(h * rows, (h + 1) * rows)
        out = jnp.where(mine[h], o[part], out)
        for i, piece in enumerate((high, middle, low)):
            side = jnp.where(lane2 == i * heads + h, piece[part], side)
    out_ref[:, :cols] = out.astype(BF)
    out_ref[:, cols:] = side.astype(BF)


def far_kernel(head_ref, qt_ref, near_ref, wo_ref, frame_ref, where_ref, *rest):
    parts, (raw_ref, s1_ref, s2_ref, s3_ref, key, value, pattern) = rest[:8], rest[8:]
    rows = qt_ref.shape[0]
    cols = qt_ref.shape[1] // 2
    heads = cols // HEAD_DIM
    each = parts[0].shape[0] * 16
    count = each * len(parts)
    for i, ref in enumerate(parts):
        spot = slice(i * each, (i + 1) * each)
        for u in range(4):
            key[u, spot, :] = ref[:, u * 16 : (u + 1) * 16, :cols].reshape(each, cols)
            value[u, spot, :] = ref[:, u * 16 : (u + 1) * 16, cols:].reshape(each, cols)
        pattern[spot, :] = ref[:, 64:, :].reshape(each, 2 * cols)
    where = where_ref[...]
    mine = (frame_ref[...] == where).astype(F32).astype(BF)
    allowed = nn(mine, pattern[...]).astype(BF)
    order = (lax.broadcasted_iota(jnp.int32, (allowed.shape[1], count), 0) == where).astype(F32).astype(BF)
    wall = jnp.where(nn(allowed, order) > 0.5, 0.0, NEG)
    q = qt_ref[:, :cols]
    lane = lax.broadcasted_iota(jnp.int32, (rows, cols), 1)
    out = jnp.zeros((rows, cols), F32)
    for h in range(heads):
        mine = (lane >= h * HEAD_DIM) & (lane < (h + 1) * HEAD_DIM)
        qh = jnp.where(mine, q, jnp.zeros_like(q))
        level = sum(near_ref[:, cols + i * heads + h : cols + i * heads + h + 1].astype(F32) for i in range(3))
        top = level
        scores = []
        for u in range(4):
            s = nt(qh, key[u]) + wall
            top = jnp.maximum(top, jnp.max(s, axis=1, keepdims=True))
            scores.append(s)
        total = jnp.exp(level - top)
        acc = total * near_ref[:, :cols].astype(F32)
        for u in range(4):
            e = jnp.exp(scores[u] - top)
            total = total + jnp.sum(e, axis=1, keepdims=True)
            acc = acc + nn(e.astype(BF), value[u])
        out = jnp.where(mine, acc / total, out)
    out = out.astype(BF)
    head = head_ref[0]
    for d, ref in ((1, s1_ref), (2, s2_ref), (3, s3_ref)):
        spot = pl.multiple_of(lax.rem(head + d, 4) * cols, 128)
        ref[...] = nn(out, wo_ref[:, pl.ds(spot, cols)]).astype(BF)
    spot = pl.multiple_of(head * cols, 128)
    raw_ref[...] = nn(out, wo_ref[:, pl.ds(spot, cols)]) + qt_ref[:, cols:].astype(F32)


def whole(n):
    return [pl.BlockSpec(memory_space=pltpu.VMEM) for _ in range(n)]


def params(mib):
    return pltpu.CompilerParams(vmem_limit_bytes=mib * 2**20)


def tm_index(z, y, c):
    return ((z % 4) * 4 + y % 4) * 2 + c


DISTANCES = (0, 1, 3, 2)
PLACES = [(z, y, c) for z in range(4) for y in range(4) for c in range(2)]
SMEM = pl.BlockSpec(memory_space=pltpu.SMEM)


def along_y(d):
    return [(tm_index(z, y, c), tm_index(z, y + d, c)) for z, y, c in PLACES]


def along_z(d):
    return [(tm_index(z, y, c), tm_index(z + d, y, c)) for z, y, c in PLACES]


OTHER_CORE = [(t, t ^ 1) for t in range(32)]


def body(tokens, w_query, w_key, w_value, w_out, pattern, visible, slot, pred):
    n_peers = lax.axis_size("tm")
    me = lax.axis_index("tm")
    head = lax.axis_index("head")
    n_heads = lax.axis_size("head")
    frames, keep = visible.shape
    width = tokens.shape[1]
    cols = w_query.shape[1]
    own = frames * keep
    steps = frames // 4
    block = 4 * PATCHES
    chunk = 4 * keep
    head_at = head.reshape(1).astype(jnp.int32)

    r = np.arange(block)
    p = r % PATCHES
    quadrant = 2 * (p // 14 >= 7) + (p % 14 >= 7)
    pool = np.zeros((16, block), np.float32)
    pool[r // PATCHES * 4 + quadrant, r] = 1.0
    n = np.arange(4 * frames)
    order = np.zeros((4 * frames, 4 * frames), np.float32)
    order[n, n % frames * 4 + n // frames] = 1.0
    pos = (jnp.arange(frames, dtype=jnp.int32)[:, None] % 4 * PATCHES + visible).reshape(own, 1)

    fixed = lambda i: (0, 0)
    mine, qt = pl.pallas_call(
        gather_kernel,
        grid=(steps,),
        in_specs=[
            SMEM,
            pl.BlockSpec((block, width), lambda i: (i, 0)),
            pl.BlockSpec((width, cols), fixed),
            pl.BlockSpec((width, cols), fixed),
            pl.BlockSpec((width, cols), fixed),
            pl.BlockSpec((16, block), fixed),
            pl.BlockSpec((chunk, 1), lambda i: (i, 0)),
            pl.BlockSpec((4 * frames, 4 * frames), fixed),
            pl.BlockSpec((frames, n_peers * frames), fixed),
        ],
        out_specs=[
            pl.BlockSpec((5 * frames, 2 * cols), fixed),
            pl.BlockSpec((own, 2 * cols), fixed),
        ],
        out_shape=[
            jax.ShapeDtypeStruct((5 * frames, 2 * cols), BF),
            jax.ShapeDtypeStruct((own, 2 * cols), BF),
        ],
        scratch_shapes=[pltpu.VMEM((4 * frames, width), F32), pltpu.VMEM((own, width), BF)],
        compiler_params=params(56),
        cost_estimate=pl.CostEstimate(flops=2 * 10**9, bytes_accessed=10**7, transcendentals=0),
        name="gather",
    )(head_at, tokens, w_query, w_key, w_value, jnp.asarray(pool, BF), pos, jnp.asarray(order, BF), pattern)

    plane = jnp.stack([mine] + [lax.ppermute(mine, "tm", along_y(d)) for d in DISTANCES[1:]])
    parts = [plane] + [lax.ppermute(plane, "tm", along_z(d)) for d in DISTANCES[1:]]
    parts = parts + [lax.ppermute(part, "tm", OTHER_CORE) for part in parts]
    my_z, my_y, my_core = me // 8, me // 2 % 4, me % 2
    gap = jnp.asarray(DISTANCES, jnp.int32)
    core_at = jnp.stack([my_core, 1 - my_core])[:, None, None, None]
    z_at = ((my_z - gap) % 4)[None, :, None, None]
    y_at = ((my_y - gap) % 4)[None, None, :, None]
    where = ((z_at * 4 + y_at) * 2 + core_at) * frames + jnp.arange(frames, dtype=jnp.int32)
    where = where.reshape(1, n_peers * frames)

    owner_all = slot // own
    my_slots = lax.dynamic_slice_in_dim(slot, me * own, own)
    my_owner = my_slots // own
    before = np.tril(np.ones((own, own), np.float32), -1)
    same = (my_owner[:, None] == my_owner[None, :]) & (before > 0)
    place = my_owner * CAP + jnp.sum(same, axis=1, dtype=jnp.int32)
    pack = (jnp.arange(n_peers * CAP, dtype=jnp.int32)[:, None] == place[None, :]).astype(BF)
    coming = (owner_all == me).reshape(n_peers, own)
    rank = jnp.dot(coming.astype(BF), jnp.asarray(before.T, BF), preferred_element_type=F32).astype(jnp.int32)
    rank = jnp.where(coming, rank, -1)
    hit = rank[:, None, :] == jnp.arange(CAP, dtype=jnp.int32)[None, :, None]
    code = (slot % own).reshape(n_peers, own) * 512 + jnp.arange(n_peers * own, dtype=jnp.int32).reshape(n_peers, own) // keep
    code = jnp.max(jnp.where(hit, code[:, None, :], -1), axis=2).reshape(1, -1)
    found = jnp.arange(own, dtype=jnp.int32)[:, None] == code >> 9
    unpack = found.astype(BF)
    frame_of = jnp.max(jnp.where(found, code & 511, 0), axis=1, keepdims=True)

    def route(x):
        packed = jnp.dot(pack, x, preferred_element_type=F32).astype(BF).reshape(n_peers, CAP, -1)
        got = lax.all_to_all(packed, "tm", 0, 0, tiled=True)
        return jnp.dot(unpack, got.reshape(n_peers * CAP, -1), preferred_element_type=F32).astype(BF)

    qt_own = route(qt)

    near = pl.pallas_call(
        near_kernel,
        grid=(steps,),
        in_specs=[
            pl.BlockSpec((chunk, cols), lambda i: (i, 0)),
            pl.BlockSpec((block, width), lambda i: (i, 0)),
            pl.BlockSpec((width, cols), fixed),
            pl.BlockSpec((width, cols), fixed),
        ],
        out_specs=pl.BlockSpec((chunk, cols + 128), lambda i: (i, 0)),
        out_shape=jax.ShapeDtypeStruct((own, cols + 128), BF),
        compiler_params=params(56),
        cost_estimate=pl.CostEstimate(flops=5 * 10**9, bytes_accessed=10**7, transcendentals=10**6),
        name="near",
    )(qt, tokens, w_key, w_value)
    near_own = route(near)

    raw, *sends = pl.pallas_call(
        far_kernel,
        in_specs=[SMEM] + whole(13),
        out_specs=whole(4),
        out_shape=[jax.ShapeDtypeStruct((own, cols), F32)] + [jax.ShapeDtypeStruct((own, cols), BF)] * 3,
        scratch_shapes=[
            pltpu.VMEM((4, n_peers * frames, cols), BF),
            pltpu.VMEM((4, n_peers * frames, cols), BF),
            pltpu.VMEM((n_peers * frames, n_peers * frames), BF),
        ],
        compiler_params=params(48),
        cost_estimate=pl.CostEstimate(flops=4 * 10**9, bytes_accessed=4 * 10**6, transcendentals=3 * 10**6),
        name="far",
    )(head_at, qt_own, near_own, w_out, frame_of, where, *parts)

    def to(d):
        return [(h, (h + d) % n_heads) for h in range(n_heads)]

    for d in (1, 3, 2):
        raw = raw + lax.ppermute(sends[d - 1], "head", to(d)).astype(F32)
    guess = pred.astype(F32)
    stats = jnp.stack([
        jnp.sum(raw, axis=1),
        jnp.sum(raw * raw, axis=1),
        jnp.sum(guess * raw, axis=1),
        jnp.sum(guess, axis=1),
        jnp.sum(guess * guess, axis=1),
    ])
    total = stats
    for d in (1, 3, 2):
        total = total + lax.ppermute(stats, "head", to(d))
    mean = total[0] / width
    var = total[1] / width - mean * mean
    scale = lax.rsqrt(var + EPS)
    normed = (raw - mean[:, None]) * scale[:, None]
    cross = (total[2] - mean * total[3]) * scale
    square = (total[1] - 2.0 * mean * total[0] + width * mean * mean) * scale * scale
    row_loss = (total[4] - 2.0 * cross + square) / width
    return normed.astype(BF), row_loss


def solution(mesh):
    return jax.shard_map(
        body,
        mesh=mesh,
        in_specs=(
            P("tm", None),
            P(None, "head"),
            P(None, "head"),
            P(None, "head"),
            P("head", None),
            P("tm", None),
            P("tm", None),
            P(),
            P("tm", "head"),
        ),
        out_specs=(P("tm", "head"), P("tm")),
        check_vma=False,
    )
```

```python
import numpy as np

import jax
import jax.numpy as jnp
from jax import lax
from jax.experimental import pallas as pl
from jax.experimental.pallas import tpu as pltpu
from jax.sharding import PartitionSpec as P

HEAD_DIM = 64
PATCHES = 196
CAP = 48
NEG = -1e30
EPS = 1e-06
BF = jnp.bfloat16
F32 = jnp.float32


def nt(a, b):
    return lax.dot_general(a, b, (((1,), (1,)), ((), ())), preferred_element_type=F32)


def nn(a, b):
    return lax.dot_general(a, b, (((1,), (0,)), ((), ())), preferred_element_type=F32)


def gather_kernel(head_ref, x_ref, wq_ref, wk_ref, wv_ref, pool_ref, vis_ref, order_ref, chunk_ref, q_ref, t_ref, sums, rows_in):
    step = pl.program_id(0)
    rows = x_ref.shape[0]
    frames, keep = vis_ref.shape
    count = 4 * keep
    cols = wk_ref.shape[1]
    x = x_ref[...]
    r = lax.broadcasted_iota(jnp.int32, (count, 1), 0)
    frame = sum((r >= keep * i).astype(jnp.int32) for i in (1, 2, 3))
    mine = (lax.broadcasted_iota(jnp.int32, (count, frames), 1) == frame + step * 4).astype(F32).astype(BF)
    seen = nn(mine, vis_ref[...].astype(F32).astype(BF))
    spot = lax.broadcasted_iota(jnp.int32, (count, keep), 1) == r - keep * frame
    pos = jnp.sum(jnp.where(spot, seen, 0.0), axis=1, keepdims=True).astype(jnp.int32) + frame * PATCHES
    pick = (pos == lax.broadcasted_iota(jnp.int32, (count, rows), 1)).astype(F32).astype(BF)
    both = nn(jnp.concatenate([pool_ref[...], pick], axis=0), x)
    sums[pl.ds(pl.multiple_of(step * 16, 16), 16), :] = both[:16]
    rows_in[pl.ds(pl.multiple_of(step * count, 16), count), :] = both[16:].astype(BF)

    @pl.when(step == pl.num_programs(0) - 1)
    def _():
        total = sums[...]
        count = total.shape[0]
        high = total.astype(BF)
        low = (total - high.astype(F32)).astype(BF)
        pair = jnp.concatenate([high, low], axis=0)
        order = order_ref[...]
        for i, w_ref in enumerate((wk_ref, wv_ref)):
            field = nn(pair, w_ref[...])
            pooled = ((field[:count] + field[count:]) / 7.0).astype(BF)
            chunk_ref[:, i * cols : (i + 1) * cols] = nn(order, pooled).astype(BF)
        q = nn(rows_in[...], wq_ref[...]).astype(BF).astype(F32) * HEAD_DIM ** -0.5
        q_ref[...] = q.astype(BF)
        t_ref[...] = rows_in[:, pl.ds(pl.multiple_of(head_ref[0] * cols, 128), cols)]


def near_kernel(q_ref, x_ref, wk_ref, wv_ref, spread_ref, q4_ref, o_ref, level_ref):
    x = x_ref[...]
    k = nn(x, wk_ref[...]).astype(BF)
    v = nn(x, wv_ref[...]).astype(BF)
    keep = q_ref.shape[0] // 4
    cols = q_ref.shape[1]
    heads = cols // HEAD_DIM
    rows = keep * heads
    r = lax.broadcasted_iota(jnp.int32, (4 * rows, cols), 0)
    lane = lax.broadcasted_iota(jnp.int32, (4 * rows, cols), 1)
    mine = lane // HEAD_DIM == r // keep % heads
    stack = jnp.where(mine, nn(spread_ref[...], q_ref[...]), 0.0).astype(BF)
    q4_ref[...] = stack
    span = 208
    for f in range(4):
        start = f * PATCHES // 16 * 16
        part = slice(f * rows, (f + 1) * rows)
        c = lax.broadcasted_iota(jnp.int32, (rows, span), 1) + (start - f * PATCHES)
        s = jnp.where((c >= 0) & (c < PATCHES), nt(stack[part], k[start : start + span]), NEG)
        m = jnp.max(s, axis=1, keepdims=True)
        e = jnp.exp(s - m)
        total = jnp.sum(e, axis=1, keepdims=True)
        o_ref[part, :] = nn(e.astype(BF), v[start : start + span]) / total
        level_ref[part, :] = jnp.broadcast_to(m + jnp.log(total), (rows, 128))


def far_kernel(q4_ref, near_ref, level_ref, allow_ref, pick_ref, where_ref, join_ref, pack_ref, *rest):
    parts, (out_ref, key, value, done) = rest[:8], rest[8:]
    cols = q4_ref.shape[1]
    heads = cols // HEAD_DIM
    each = parts[0].shape[0] * 16
    count = each * len(parts)
    for i, ref in enumerate(parts):
        spot = slice(i * each, (i + 1) * each)
        for u in range(4):
            key[u, spot, :] = ref[:, u * 16 : (u + 1) * 16, :cols].reshape(each, cols)
            value[u, spot, :] = ref[:, u * 16 : (u + 1) * 16, cols:].reshape(each, cols)
    allowed = allow_ref[...].astype(F32).astype(BF)
    order = (lax.broadcasted_iota(jnp.int32, (allowed.shape[1], count), 0) == where_ref[...]).astype(F32).astype(BF)
    wall = jnp.where(nn(allowed, order) > 0.5, 0.0, NEG).astype(BF)
    rows = q4_ref.shape[0] // 4
    keep = rows // 4 // heads
    r = lax.broadcasted_iota(jnp.int32, (rows, cols), 0)
    mine = lax.broadcasted_iota(jnp.int32, (rows, cols), 1) // HEAD_DIM == r // keep % heads
    for g in range(4):
        part = slice(g * rows, (g + 1) * rows)
        block = nn(pick_ref[part, :], wall)
        q = q4_ref[part, :]
        level = level_ref[part, :1]
        top = level
        scores = []
        for u in range(4):
            s = nt(q, key[u]) + block
            top = jnp.maximum(top, jnp.max(s, axis=1, keepdims=True))
            scores.append(s)
        total = jnp.exp(level - top)
        acc = total * near_ref[part, :]
        for u in range(4):
            e = jnp.exp(scores[u] - top)
            total = total + jnp.sum(e, axis=1, keepdims=True)
            acc = acc + nn(e.astype(BF), value[u])
        done[part, :] = jnp.where(mine, acc / total, 0.0).astype(BF)
    out = nn(join_ref[...], done[...]).astype(BF)
    out_ref[...] = nn(pack_ref[...], out).astype(BF).reshape(out_ref.shape)


def final_kernel(head_ref, wo_ref, *rest):
    att, side, (target_ref, loss_ref, raw) = rest[:4], rest[4:8], rest[8:]
    head = head_ref[0]
    rows, cols = att[0].shape
    width = raw.shape[1]
    raw[...] = sum(nn(att[i][...], wo_ref[i]) for i in range(4))
    spots = [pl.ds(pl.multiple_of(lax.rem(head + 4 - d, 4) * cols, 128), cols) for d in DISTANCES]
    for i in range(4):
        raw[:, spots[i]] += side[i][:, :cols].astype(F32)
    full = raw[...]
    mean = jnp.sum(full, axis=1, keepdims=True) / width
    var = jnp.sum(full * full, axis=1, keepdims=True) / width - mean * mean
    scale = lax.rsqrt(var + EPS)
    loss = jnp.zeros((rows, 1), F32)
    for i in range(4):
        normed = (raw[:, spots[i]] - mean) * scale
        if i == 0:
            target_ref[...] = normed.astype(BF)
        gap = side[i][:, cols:].astype(F32) - normed
        loss = loss + jnp.sum(gap * gap, axis=1, keepdims=True)
    loss_ref[...] = jnp.broadcast_to(loss / width, (rows, 128)).T[:1]


def whole(n):
    return [pl.BlockSpec(memory_space=pltpu.VMEM) for _ in range(n)]


def params(mib):
    return pltpu.CompilerParams(vmem_limit_bytes=mib * 2**20)


def tm_index(z, y, c):
    return ((z % 4) * 4 + y % 4) * 2 + c


DISTANCES = (0, 1, 3, 2)
PLACES = [(z, y, c) for z in range(4) for y in range(4) for c in range(2)]
SMEM = pl.BlockSpec(memory_space=pltpu.SMEM)


def along_y(d):
    return [(tm_index(z, y, c), tm_index(z, y + d, c)) for z, y, c in PLACES]


def along_z(d):
    return [(tm_index(z, y, c), tm_index(z + d, y, c)) for z, y, c in PLACES]


OTHER_CORE = [(t, t ^ 1) for t in range(32)]


def body(tokens, w_query, w_key, w_value, w_out, pattern, visible, slot, pred):
    n_peers = lax.axis_size("tm")
    me = lax.axis_index("tm")
    head = lax.axis_index("head")
    n_heads = lax.axis_size("head")
    frames, keep = visible.shape
    width = tokens.shape[1]
    cols = w_query.shape[1]
    own = frames * keep
    steps = frames // 4
    block = 4 * PATCHES
    chunk = 4 * keep
    head_at = head.reshape(1).astype(jnp.int32)

    r = np.arange(block)
    p = r % PATCHES
    quadrant = 2 * (p // 14 >= 7) + (p % 14 >= 7)
    pool = np.zeros((16, block), np.float32)
    pool[r // PATCHES * 4 + quadrant, r] = 1.0
    n = np.arange(4 * frames)
    order = np.zeros((4 * frames, 4 * frames), np.float32)
    order[n, n % frames * 4 + n // frames] = 1.0

    fixed = lambda i: (0, 0)
    mine, q, tok = pl.pallas_call(
        gather_kernel,
        grid=(steps,),
        in_specs=[
            SMEM,
            pl.BlockSpec((block, width), lambda i: (i, 0)),
            pl.BlockSpec((width, cols), fixed),
            pl.BlockSpec((width, cols), fixed),
            pl.BlockSpec((width, cols), fixed),
            pl.BlockSpec((16, block), fixed),
            pl.BlockSpec((frames, keep), fixed),
            pl.BlockSpec((4 * frames, 4 * frames), fixed),
        ],
        out_specs=[
            pl.BlockSpec((4 * frames, 2 * cols), fixed),
            pl.BlockSpec((own, cols), fixed),
            pl.BlockSpec((own, cols), fixed),
        ],
        out_shape=[
            jax.ShapeDtypeStruct((4 * frames, 2 * cols), BF),
            jax.ShapeDtypeStruct((own, cols), BF),
            jax.ShapeDtypeStruct((own, cols), BF),
        ],
        scratch_shapes=[pltpu.VMEM((4 * frames, width), F32), pltpu.VMEM((own, width), BF)],
        compiler_params=params(56),
        cost_estimate=pl.CostEstimate(flops=2 * 10**9, bytes_accessed=10**7, transcendentals=0),
        name="gather",
    )(head_at, tokens, w_query, w_key, w_value, jnp.asarray(pool, BF), visible, jnp.asarray(order, BF))

    plane = jnp.stack([mine] + [lax.ppermute(mine, "tm", along_y(d)) for d in DISTANCES[1:]])
    plane, q, tok = lax.optimization_barrier((plane, q, tok))
    parts = [plane] + [lax.ppermute(plane, "tm", along_z(d)) for d in DISTANCES[1:]]
    my_z, my_y, my_core = me // 8, me // 2 % 4, me % 2
    gap = jnp.asarray(DISTANCES, jnp.int32)
    core_at = jnp.stack([my_core, 1 - my_core])[:, None, None, None]
    z_at = ((my_z - gap) % 4)[None, :, None, None]
    y_at = ((my_y - gap) % 4)[None, None, :, None]
    where = ((z_at * 4 + y_at) * 2 + core_at) * frames + jnp.arange(frames, dtype=jnp.int32)
    where = where.reshape(1, n_peers * frames)

    owner_all = slot // own
    my_slots = lax.dynamic_slice_in_dim(slot, me * own, own)
    my_owner = my_slots // own
    before = np.tril(np.ones((own, own), np.float32), -1)
    same = (my_owner[:, None] == my_owner[None, :]) & (before > 0)
    place = my_owner * CAP + jnp.sum(same, axis=1, dtype=jnp.int32)
    pack = (jnp.arange(n_peers * CAP, dtype=jnp.int32)[:, None] == place[None, :]).astype(BF)
    coming = (owner_all == me).reshape(n_peers, own)
    rank = jnp.dot(coming.astype(BF), jnp.asarray(before.T, BF), preferred_element_type=F32).astype(jnp.int32)
    rank = jnp.where(coming, rank, -1)
    hit = rank[:, None, :] == jnp.arange(CAP, dtype=jnp.int32)[None, :, None]
    student = jnp.max(jnp.where(hit, (slot % own).reshape(n_peers, 1, own), -1), axis=2)
    unpack = (jnp.arange(own, dtype=jnp.int32)[:, None] == student.reshape(1, -1)).astype(BF)

    def deliver(packed):
        return lax.all_to_all(packed, "tm", 0, 0, tiled=True)

    def arrange(got):
        return jnp.dot(unpack, got.reshape(n_peers * CAP, -1), preferred_element_type=F32).astype(BF)

    tok_got = deliver(jnp.dot(pack, tok, preferred_element_type=F32).astype(BF).reshape(n_peers, CAP, cols))

    heads = cols // HEAD_DIM
    n = np.arange(own * heads)
    n_frame, n_keep = n // (keep * heads), n % keep
    spread = jnp.asarray(n_frame[: chunk * heads, None] * keep + n_keep[: chunk * heads, None] == np.arange(chunk), BF)
    pick = jnp.asarray(n_frame[:, None] == np.arange(frames), BF)
    join = jnp.asarray(np.arange(own)[:, None] == n_frame * keep + n_keep, BF)
    q4, near, level = pl.pallas_call(
        near_kernel,
        grid=(steps,),
        in_specs=[
            pl.BlockSpec((chunk, cols), lambda i: (i, 0)),
            pl.BlockSpec((block, width), lambda i: (i, 0)),
            pl.BlockSpec((width, cols), fixed),
            pl.BlockSpec((width, cols), fixed),
            pl.BlockSpec((chunk * heads, chunk), fixed),
        ],
        out_specs=[
            pl.BlockSpec((chunk * heads, cols), lambda i: (i, 0)),
            pl.BlockSpec((chunk * heads, cols), lambda i: (i, 0)),
            pl.BlockSpec((chunk * heads, 128), lambda i: (i, 0)),
        ],
        out_shape=[
            jax.ShapeDtypeStruct((own * heads, cols), BF),
            jax.ShapeDtypeStruct((own * heads, cols), F32),
            jax.ShapeDtypeStruct((own * heads, 128), F32),
        ],
        compiler_params=params(56),
        cost_estimate=pl.CostEstimate(flops=5 * 10**9, bytes_accessed=10**7, transcendentals=10**6),
        name="near",
    )(q, tokens, w_key, w_value, spread)

    q4, w_out = lax.optimization_barrier((q4, w_out))
    *parts, q4, near, level, tok_got = lax.optimization_barrier((*parts, q4, near, level, tok_got))
    parts = parts + [lax.ppermute(part, "tm", OTHER_CORE) for part in parts]
    packed = pl.pallas_call(
        far_kernel,
        in_specs=whole(16),
        out_specs=pl.BlockSpec(memory_space=pltpu.VMEM),
        out_shape=jax.ShapeDtypeStruct((n_peers, CAP, cols), BF),
        scratch_shapes=[
            pltpu.VMEM((4, n_peers * frames, cols), BF),
            pltpu.VMEM((4, n_peers * frames, cols), BF),
            pltpu.VMEM((own * heads, cols), BF),
        ],
        compiler_params=params(40),
        cost_estimate=pl.CostEstimate(flops=4 * 10**9, bytes_accessed=4 * 10**6, transcendentals=3 * 10**6),
        name="far",
    )(q4, near, level, pattern, pick, where, join, pack, *parts)
    packed, tok_got = lax.optimization_barrier((packed, tok_got))
    tok_own = arrange(tok_got)
    att = arrange(deliver(packed))

    def to(d):
        return [(h, (h + d) % n_heads) for h in range(n_heads)]

    def over_heads(x):
        return [x] + [lax.ppermute(x, "head", to(d)) for d in DISTANCES[1:]]

    half = cols // 2
    halves = jnp.stack(over_heads(lax.dynamic_slice_in_dim(w_out, my_core * half, half, 0)))
    other = lax.ppermute(halves, "tm", OTHER_CORE)
    first = my_core == 0
    w_all = jnp.concatenate([jnp.where(first, halves, other), jnp.where(first, other, halves)], axis=1)
    side = over_heads(jnp.concatenate([tok_own, pred], axis=1))

    target, row_loss = pl.pallas_call(
        final_kernel,
        in_specs=[SMEM] + whole(9),
        out_specs=whole(2),
        out_shape=[jax.ShapeDtypeStruct((own, cols), BF), jax.ShapeDtypeStruct((1, own), F32)],
        scratch_shapes=[pltpu.VMEM((own, width), F32)],
        compiler_params=params(40),
        cost_estimate=pl.CostEstimate(flops=10**9, bytes_accessed=4 * 10**6, transcendentals=0),
        name="final",
    )(head_at, w_all, *over_heads(att), *side)
    return target, row_loss.reshape(own)


def solution(mesh):
    return jax.shard_map(
        body,
        mesh=mesh,
        in_specs=(
            P("tm", None),
            P(None, "head"),
            P(None, "head"),
            P(None, "head"),
            P("head", None),
            P("tm", None),
            P("tm", None),
            P(),
            P("tm", "head"),
        ),
        out_specs=(P("tm", "head"), P("tm")),
        check_vma=False,
    )
```

```python
import numpy as np

import jax
import jax.numpy as jnp
from jax import lax
from jax.experimental import pallas as pl
from jax.experimental.pallas import tpu as pltpu
from jax.sharding import PartitionSpec as P

HEAD_DIM = 64
PATCHES = 196
CAP = 48
NEG = -1e30
EPS = 1e-06
BF = jnp.bfloat16
F32 = jnp.float32


def nt(a, b):
    return lax.dot_general(a, b, (((1,), (1,)), ((), ())), preferred_element_type=F32)


def nn(a, b):
    return lax.dot_general(a, b, (((1,), (0,)), ((), ())), preferred_element_type=F32)


def fetch(pairs, sem):
    copies = [pltpu.make_async_copy(source, target, sem.at[i]) for i, (source, target) in enumerate(pairs)]
    for copy in copies:
        copy.start()
    return copies


def row_blocks(ref, count):
    size = ref.shape[0] // count
    return [ref.at[pl.ds(i * size, size)] for i in range(count)]


def gather_kernel(
    head_ref, x_hbm, wq_hbm, wk_hbm, wv_hbm, pool_ref, vis_ref, order_ref, chunk_ref, q_ref, t_ref, x_ref, wq_ref, wk_ref, wv_ref, sums, rows_in, sem
):
    steps = vis_ref.shape[0] // 4
    pairs = list(zip(row_blocks(x_hbm, steps), row_blocks(x_ref, steps)))
    copies = fetch(pairs + [(wk_hbm, wk_ref), (wv_hbm, wv_ref), (wq_hbm, wq_ref)], sem)
    rows = x_ref.shape[0] // steps
    frames, keep = vis_ref.shape
    count = 4 * keep
    cols = wk_ref.shape[1]
    r = lax.broadcasted_iota(jnp.int32, (count, 1), 0)
    frame = sum((r >= keep * i).astype(jnp.int32) for i in (1, 2, 3))
    spot = lax.broadcasted_iota(jnp.int32, (count, keep), 1) == r - keep * frame
    for step in range(steps):
        mine = (lax.broadcasted_iota(jnp.int32, (count, frames), 1) == frame + step * 4).astype(F32).astype(BF)
        seen = nn(mine, vis_ref[...].astype(F32).astype(BF))
        pos = jnp.sum(jnp.where(spot, seen, 0.0), axis=1, keepdims=True).astype(jnp.int32) + frame * PATCHES
        pick = (pos == lax.broadcasted_iota(jnp.int32, (count, rows), 1)).astype(F32).astype(BF)
        choose = jnp.concatenate([pool_ref[...], pick], axis=0)
        copies[step].wait()
        both = nn(choose, x_ref[step * rows : (step + 1) * rows, :])
        sums[step * 16 : (step + 1) * 16, :] = both[:16]
        rows_in[step * count : (step + 1) * count, :] = both[16:].astype(BF)
    total = sums[...]
    count = total.shape[0]
    high = total.astype(BF)
    low = (total - high.astype(F32)).astype(BF)
    pair = jnp.concatenate([high, low], axis=0)
    order = order_ref[...]
    for i, w_ref in enumerate((wk_ref, wv_ref)):
        copies[steps + i].wait()
        field = nn(pair, w_ref[...])
        pooled = ((field[:count] + field[count:]) / 7.0).astype(BF)
        chunk_ref[:, i * cols : (i + 1) * cols] = nn(order, pooled).astype(BF)
    copies[steps + 2].wait()
    q = nn(rows_in[...], wq_ref[...]).astype(BF).astype(F32) * HEAD_DIM ** -0.5
    q_ref[...] = q.astype(BF)
    t_ref[...] = rows_in[:, pl.ds(pl.multiple_of(head_ref[0] * cols, 128), cols)]


def stacked(q, spread, keep, heads):
    rows, cols = spread.shape[0], q.shape[1]
    r = lax.broadcasted_iota(jnp.int32, (rows, cols), 0)
    lane = lax.broadcasted_iota(jnp.int32, (rows, cols), 1)
    mine = lane // HEAD_DIM == r // keep % heads
    return mine, jnp.where(mine, nn(spread, q), 0.0).astype(BF)


def near_kernel(q_ref, x_hbm, wk_hbm, wv_hbm, spread_ref, out_ref, x_ref, wk_ref, wv_ref, sem):
    heads = wk_ref.shape[1] // HEAD_DIM
    chunk = spread_ref.shape[1]
    steps = q_ref.shape[0] // chunk
    pairs = list(zip(row_blocks(x_hbm, steps), row_blocks(x_ref, steps)))
    copies = fetch([(wk_hbm, wk_ref), (wv_hbm, wv_ref)] + pairs, sem)
    size = x_ref.shape[0] // steps
    keep = chunk // 4
    cols = q_ref.shape[1]
    rows = keep * heads
    span = 208
    lane = lax.broadcasted_iota(jnp.int32, (rows, 128), 1)
    copies[0].wait()
    copies[1].wait()
    for step in range(steps):
        copies[2 + step].wait()
        x = x_ref[step * size : (step + 1) * size, :]
        k = nn(x, wk_ref[...]).astype(BF)
        v = nn(x, wv_ref[...]).astype(BF)
        _, stack = stacked(q_ref[step * chunk : (step + 1) * chunk, :], spread_ref[...], keep, heads)
        for f in range(4):
            start = f * PATCHES // 16 * 16
            part = slice((step * 4 + f) * rows, (step * 4 + f + 1) * rows)
            c = lax.broadcasted_iota(jnp.int32, (rows, span), 1) + (start - f * PATCHES)
            s = jnp.where((c >= 0) & (c < PATCHES), nt(stack[f * rows : (f + 1) * rows], k[start : start + span]), NEG)
            m = jnp.max(s, axis=1, keepdims=True)
            e = jnp.exp(s - m)
            total = jnp.sum(e, axis=1, keepdims=True)
            level = m + jnp.log(total)
            high = level.astype(BF).astype(F32)
            middle = (level - high).astype(BF).astype(F32)
            side = jnp.where(lane == 0, high, jnp.where(lane == 1, middle, level - high - middle))
            out_ref[part, :cols] = (nn(e.astype(BF), v[start : start + span]) / total).astype(BF)
            out_ref[part, cols:] = side.astype(BF)


def far_kernel(q_ref, near_ref, allow_ref, pick_ref, where_ref, spread_ref, pack_ref, *rest):
    parts, (out_ref, key, value) = rest[:8], rest[8:]
    cols = q_ref.shape[1]
    heads = cols // HEAD_DIM
    chunk = spread_ref.shape[1]
    each = parts[0].shape[0] * 16
    count = each * len(parts)
    for i, ref in enumerate(parts):
        spot = slice(i * each, (i + 1) * each)
        for u in range(4):
            key[u, spot, :] = ref[:, u * 16 : (u + 1) * 16, :cols].reshape(each, cols)
            value[u, spot, :] = ref[:, u * 16 : (u + 1) * 16, cols:].reshape(each, cols)
    allowed = allow_ref[...].astype(F32).astype(BF)
    order = (lax.broadcasted_iota(jnp.int32, (allowed.shape[1], count), 0) == where_ref[...]).astype(F32).astype(BF)
    wall = jnp.where(nn(allowed, order) > 0.5, 0.0, NEG).astype(BF)
    rows = spread_ref.shape[0]
    outs = []
    for g in range(q_ref.shape[0] // chunk):
        part = slice(g * rows, (g + 1) * rows)
        mine, q = stacked(q_ref[g * chunk : (g + 1) * chunk, :], spread_ref[...], chunk // 4, heads)
        block = nn(pick_ref[part, :], wall)
        level = sum(near_ref[part, cols + i : cols + i + 1].astype(F32) for i in range(3))
        top = level
        scores = []
        for u in range(4):
            s = nt(q, key[u]) + block
            top = jnp.maximum(top, jnp.max(s, axis=1, keepdims=True))
            scores.append(s)
        total = jnp.exp(level - top)
        acc = total * near_ref[part, :cols].astype(F32)
        for u in range(4):
            e = jnp.exp(scores[u] - top)
            total = total + jnp.sum(e, axis=1, keepdims=True)
            acc = acc + nn(e.astype(BF), value[u])
        done = jnp.where(mine, acc / total, 0.0).astype(BF)
        outs.append(lax.dot_general(spread_ref[...], done, (((0,), (0,)), ((), ())), preferred_element_type=F32).astype(BF))
    out = jnp.concatenate(outs, axis=0)
    out_ref[...] = nn(pack_ref[...], out).astype(BF).reshape(out_ref.shape)


def final_kernel(at_ref, *rest):
    att, side, own_half, other_half, (target_ref, loss_ref, raw) = rest[:4], rest[4:8], rest[8:12], rest[12:16], rest[16:]
    head, core = at_ref[0], at_ref[1]
    rows, cols = att[0].shape
    half = cols // 2
    width = raw.shape[1]
    here = pl.ds(pl.multiple_of(core * half, 128), half)
    there = pl.ds(pl.multiple_of((1 - core) * half, 128), half)
    raw[...] = sum(nn(att[i][:, here], own_half[i][...]) + nn(att[i][:, there], other_half[i][...]) for i in range(4))
    spots = [pl.ds(pl.multiple_of(lax.rem(head + 4 - d, 4) * cols, 128), cols) for d in DISTANCES]
    for i in range(4):
        raw[:, spots[i]] += side[i][:, :cols].astype(F32)
    full = raw[...]
    mean = jnp.sum(full, axis=1, keepdims=True) / width
    var = jnp.sum(full * full, axis=1, keepdims=True) / width - mean * mean
    scale = lax.rsqrt(var + EPS)
    loss = jnp.zeros((rows, 1), F32)
    for i in range(4):
        normed = (raw[:, spots[i]] - mean) * scale
        if i == 0:
            target_ref[...] = normed.astype(BF)
        gap = side[i][:, cols:].astype(F32) - normed
        loss = loss + jnp.sum(gap * gap, axis=1, keepdims=True)
    loss_ref[...] = jnp.broadcast_to(loss / width, (rows, 128)).T[:1]


def whole(n):
    return [pl.BlockSpec(memory_space=pltpu.VMEM) for _ in range(n)]


def params(mib):
    return pltpu.CompilerParams(vmem_limit_bytes=mib * 2**20)


def tm_index(z, y, c):
    return ((z % 4) * 4 + y % 4) * 2 + c


DISTANCES = (0, 1, 3, 2)
PLACES = [(z, y, c) for z in range(4) for y in range(4) for c in range(2)]
SMEM = pl.BlockSpec(memory_space=pltpu.SMEM)
HBM = pl.BlockSpec(memory_space=pl.ANY)


def along_y(d):
    return [(tm_index(z, y, c), tm_index(z, y + d, c)) for z, y, c in PLACES]


def along_z(d):
    return [(tm_index(z, y, c), tm_index(z + d, y, c)) for z, y, c in PLACES]


OTHER_CORE = [(t, t ^ 1) for t in range(32)]


def body(tokens, w_query, w_key, w_value, w_out, pattern, visible, slot, pred):
    n_peers = lax.axis_size("tm")
    me = lax.axis_index("tm")
    head = lax.axis_index("head")
    n_heads = lax.axis_size("head")
    frames, keep = visible.shape
    width = tokens.shape[1]
    cols = w_query.shape[1]
    own = frames * keep
    steps = frames // 4
    block = 4 * PATCHES
    chunk = 4 * keep
    my_z, my_y, my_core = me // 8, me // 2 % 4, me % 2
    at = jnp.stack([head, my_core]).astype(jnp.int32)

    r = np.arange(block)
    p = r % PATCHES
    quadrant = 2 * (p // 14 >= 7) + (p % 14 >= 7)
    pool = np.zeros((16, block), np.float32)
    pool[r // PATCHES * 4 + quadrant, r] = 1.0
    n = np.arange(4 * frames)
    order = np.zeros((4 * frames, 4 * frames), np.float32)
    order[n, n % frames * 4 + n // frames] = 1.0

    mine, q, tok = pl.pallas_call(
        gather_kernel,
        in_specs=[SMEM] + [HBM] * 4 + whole(3),
        out_specs=whole(3),
        out_shape=[
            jax.ShapeDtypeStruct((4 * frames, 2 * cols), BF),
            jax.ShapeDtypeStruct((own, cols), BF),
            jax.ShapeDtypeStruct((own, cols), BF),
        ],
        scratch_shapes=[pltpu.VMEM((frames * PATCHES, width), BF)]
        + [pltpu.VMEM((width, cols), BF)] * 3
        + [pltpu.VMEM((4 * frames, width), F32), pltpu.VMEM((own, width), BF), pltpu.SemaphoreType.DMA((steps + 3,))],
        compiler_params=params(56),
        cost_estimate=pl.CostEstimate(flops=2 * 10**9, bytes_accessed=10**7, transcendentals=0),
        name="gather",
    )(at, tokens, w_query, w_key, w_value, jnp.asarray(pool, BF), visible, jnp.asarray(order, BF))

    plane = jnp.stack([mine] + [lax.ppermute(mine, "tm", along_y(d)) for d in DISTANCES[1:]])
    plane, q, tok = lax.optimization_barrier((plane, q, tok))
    parts = [plane] + [lax.ppermute(plane, "tm", along_z(d)) for d in DISTANCES[1:]]
    gap = jnp.asarray(DISTANCES, jnp.int32)
    core_at = jnp.stack([my_core, 1 - my_core])[:, None, None, None]
    z_at = ((my_z - gap) % 4)[None, :, None, None]
    y_at = ((my_y - gap) % 4)[None, None, :, None]
    where = ((z_at * 4 + y_at) * 2 + core_at) * frames + jnp.arange(frames, dtype=jnp.int32)
    where = where.reshape(1, n_peers * frames)

    owner_all = slot // own
    my_slots = lax.dynamic_slice_in_dim(slot, me * own, own)
    my_owner = my_slots // own
    before = np.tril(np.ones((own, own), np.float32), -1)
    same = (my_owner[:, None] == my_owner[None, :]) & (before > 0)
    place = my_owner * CAP + jnp.sum(same, axis=1, dtype=jnp.int32)
    pack = (jnp.arange(n_peers * CAP, dtype=jnp.int32)[:, None] == place[None, :]).astype(BF)
    coming = (owner_all == me).reshape(n_peers, own)
    rank = jnp.dot(coming.astype(BF), jnp.asarray(before.T, BF), preferred_element_type=F32).astype(jnp.int32)
    rank = jnp.where(coming, rank, -1)
    hit = rank[:, None, :] == jnp.arange(CAP, dtype=jnp.int32)[None, :, None]
    student = jnp.max(jnp.where(hit, (slot % own).reshape(n_peers, 1, own), -1), axis=2)
    unpack = (jnp.arange(own, dtype=jnp.int32)[:, None] == student.reshape(1, -1)).astype(BF)

    def deliver(packed):
        return lax.all_to_all(packed, "tm", 0, 0, tiled=True)

    def arrange(got):
        return jnp.dot(unpack, got.reshape(n_peers * CAP, -1), preferred_element_type=F32).astype(BF)

    tok_got = deliver(jnp.dot(pack, tok, preferred_element_type=F32).astype(BF).reshape(n_peers, CAP, cols))

    heads = cols // HEAD_DIM
    n = np.arange(own * heads)
    n_frame, n_keep = n // (keep * heads), n % keep
    spread = jnp.asarray(n_frame[: chunk * heads, None] * keep + n_keep[: chunk * heads, None] == np.arange(chunk), BF)
    pick = jnp.asarray(n_frame[:, None] == np.arange(frames), BF)
    near = pl.pallas_call(
        near_kernel,
        in_specs=whole(1) + [HBM] * 3 + whole(1),
        out_specs=pl.BlockSpec(memory_space=pltpu.VMEM),
        out_shape=jax.ShapeDtypeStruct((own * heads, cols + 128), BF),
        scratch_shapes=[pltpu.VMEM((frames * PATCHES, width), BF)]
        + [pltpu.VMEM((width, cols), BF)] * 2
        + [pltpu.SemaphoreType.DMA((steps + 2,))],
        compiler_params=params(40),
        cost_estimate=pl.CostEstimate(flops=5 * 10**9, bytes_accessed=10**7, transcendentals=10**6),
        name="near",
    )(q, tokens, w_key, w_value, spread)

    *parts, q, near, tok_got = lax.optimization_barrier((*parts, q, near, tok_got))
    parts = parts + [lax.ppermute(part, "tm", OTHER_CORE) for part in parts]
    packed = pl.pallas_call(
        far_kernel,
        in_specs=whole(15),
        out_specs=pl.BlockSpec(memory_space=pltpu.VMEM),
        out_shape=jax.ShapeDtypeStruct((n_peers, CAP, cols), BF),
        scratch_shapes=[
            pltpu.VMEM((4, n_peers * frames, cols), BF),
            pltpu.VMEM((4, n_peers * frames, cols), BF),
        ],
        compiler_params=params(40),
        cost_estimate=pl.CostEstimate(flops=4 * 10**9, bytes_accessed=4 * 10**6, transcendentals=3 * 10**6),
        name="far",
    )(q, near, pattern, pick, where, spread, pack, *parts)
    packed, tok_got = lax.optimization_barrier((packed, tok_got))
    tok_own = arrange(tok_got)
    att = arrange(deliver(packed))

    def to(d):
        return [(h, (h + d) % n_heads) for h in range(n_heads)]

    def over_heads(x):
        return [x] + [lax.ppermute(x, "head", to(d)) for d in DISTANCES[1:]]

    half = cols // 2
    halves = over_heads(lax.dynamic_slice_in_dim(w_out, my_core * half, half, 0))
    other = [lax.ppermute(piece, "tm", OTHER_CORE) for piece in halves]
    side = over_heads(jnp.concatenate([tok_own, pred], axis=1))

    target, row_loss = pl.pallas_call(
        final_kernel,
        in_specs=[SMEM] + whole(16),
        out_specs=whole(2),
        out_shape=[jax.ShapeDtypeStruct((own, cols), BF), jax.ShapeDtypeStruct((1, own), F32)],
        scratch_shapes=[pltpu.VMEM((own, width), F32)],
        compiler_params=params(40),
        cost_estimate=pl.CostEstimate(flops=10**9, bytes_accessed=4 * 10**6, transcendentals=0),
        name="final",
    )(at, *over_heads(att), *side, *halves, *other)
    return target, row_loss.reshape(own)


def solution(mesh):
    return jax.shard_map(
        body,
        mesh=mesh,
        in_specs=(
            P("tm", None),
            P(None, "head"),
            P(None, "head"),
            P(None, "head"),
            P("head", None),
            P("tm", None),
            P("tm", None),
            P(),
            P("tm", "head"),
        ),
        out_specs=(P("tm", "head"), P("tm")),
        check_vma=False,
    )
```

```python
import numpy as np

import jax
import jax.numpy as jnp
from jax import lax
from jax.experimental import pallas as pl
from jax.experimental.pallas import tpu as pltpu
from jax.sharding import PartitionSpec as P

HEAD_DIM = 64
PATCHES = 196
CAP = 48
NEG = -1e30
EPS = 1e-06
BF = jnp.bfloat16
F32 = jnp.float32


def nt(a, b):
    return lax.dot_general(a, b, (((1,), (1,)), ((), ())), preferred_element_type=F32)


def nn(a, b):
    return lax.dot_general(a, b, (((1,), (0,)), ((), ())), preferred_element_type=F32)


def fetch(pairs, sem):
    copies = [pltpu.make_async_copy(source, target, sem.at[i]) for i, (source, target) in enumerate(pairs)]
    for copy in copies:
        copy.start()
    return copies


def row_blocks(ref, count):
    size = ref.shape[0] // count
    return [ref.at[pl.ds(i * size, size)] for i in range(count)]


def gather_kernel(
    x_hbm, wq_hbm, wk_hbm, wv_hbm, pool_ref, vis_ref, order_ref, chunk_ref, q_ref, t_ref, x_ref, wq_ref, wk_ref, wv_ref, sums, rows_in, sem
):
    steps = vis_ref.shape[0] // 4
    pairs = list(zip(row_blocks(x_hbm, steps), row_blocks(x_ref, steps)))
    copies = fetch(pairs + [(wk_hbm, wk_ref), (wv_hbm, wv_ref), (wq_hbm, wq_ref)], sem)
    rows = x_ref.shape[0] // steps
    frames, keep = vis_ref.shape
    count = 4 * keep
    cols = wk_ref.shape[1]
    r = lax.broadcasted_iota(jnp.int32, (count, 1), 0)
    frame = sum((r >= keep * i).astype(jnp.int32) for i in (1, 2, 3))
    spot = lax.broadcasted_iota(jnp.int32, (count, keep), 1) == r - keep * frame
    for step in range(steps):
        mine = (lax.broadcasted_iota(jnp.int32, (count, frames), 1) == frame + step * 4).astype(F32).astype(BF)
        seen = nn(mine, vis_ref[...].astype(F32).astype(BF))
        pos = jnp.sum(jnp.where(spot, seen, 0.0), axis=1, keepdims=True).astype(jnp.int32) + frame * PATCHES
        pick = (pos == lax.broadcasted_iota(jnp.int32, (count, rows), 1)).astype(F32).astype(BF)
        choose = jnp.concatenate([pool_ref[...], pick], axis=0)
        copies[step].wait()
        both = nn(choose, x_ref[step * rows : (step + 1) * rows, :])
        sums[step * 16 : (step + 1) * 16, :] = both[:16]
        rows_in[step * count : (step + 1) * count, :] = both[16:].astype(BF)
    total = sums[...]
    count = total.shape[0]
    high = total.astype(BF)
    low = (total - high.astype(F32)).astype(BF)
    pair = jnp.concatenate([high, low], axis=0)
    order = order_ref[...]
    for i, w_ref in enumerate((wk_ref, wv_ref)):
        copies[steps + i].wait()
        field = nn(pair, w_ref[...])
        pooled = ((field[:count] + field[count:]) / 7.0).astype(BF)
        chunk_ref[:, i * cols : (i + 1) * cols] = nn(order, pooled).astype(BF)
    copies[steps + 2].wait()
    q = nn(rows_in[...], wq_ref[...]).astype(BF).astype(F32) * HEAD_DIM ** -0.5
    q_ref[...] = q.astype(BF)
    t_ref[...] = rows_in[:, pl.ds(pl.multiple_of(lax.axis_index("head") * cols, 128), cols)]


def spreading(keep, heads):
    shape = (4 * keep * heads, 4 * keep)
    r = lax.broadcasted_iota(jnp.int32, shape, 0)
    source = r // (keep * heads) * keep + r % keep
    return (source == lax.broadcasted_iota(jnp.int32, shape, 1)).astype(F32).astype(BF)


def own_lanes(keep, heads):
    shape = (4 * keep * heads, heads * HEAD_DIM)
    r = lax.broadcasted_iota(jnp.int32, shape, 0)
    return lax.broadcasted_iota(jnp.int32, shape, 1) // HEAD_DIM == r // keep % heads


def near_kernel(q_hbm, x_hbm, wk_hbm, wv_hbm, out_ref, q_ref, x_ref, wk_ref, wv_ref, sem):
    heads = wk_ref.shape[1] // HEAD_DIM
    steps = x_ref.shape[0] // (4 * PATCHES)
    chunk = q_ref.shape[0] // steps
    pairs = list(zip(row_blocks(x_hbm, steps), row_blocks(x_ref, steps)))
    copies = fetch([(wk_hbm, wk_ref), (wv_hbm, wv_ref)] + pairs + [(q_hbm, q_ref)], sem)
    size = x_ref.shape[0] // steps
    keep = chunk // 4
    cols = q_ref.shape[1]
    rows = keep * heads
    span = 208
    lane = lax.broadcasted_iota(jnp.int32, (rows, 128), 1)
    spread = spreading(keep, heads)
    mine = own_lanes(keep, heads)
    copies[-1].wait()
    copies[0].wait()
    copies[1].wait()
    for step in range(steps):
        copies[2 + step].wait()
        x = x_ref[step * size : (step + 1) * size, :]
        k = nn(x, wk_ref[...]).astype(BF)
        v = nn(x, wv_ref[...]).astype(BF)
        stack = jnp.where(mine, nn(spread, q_ref[step * chunk : (step + 1) * chunk, :]), 0.0).astype(BF)
        for f in range(4):
            start = f * PATCHES // 16 * 16
            part = slice((step * 4 + f) * rows, (step * 4 + f + 1) * rows)
            c = lax.broadcasted_iota(jnp.int32, (rows, span), 1) + (start - f * PATCHES)
            s = jnp.where((c >= 0) & (c < PATCHES), nt(stack[f * rows : (f + 1) * rows], k[start : start + span]), NEG)
            m = jnp.max(s, axis=1, keepdims=True)
            e = jnp.exp(s - m)
            total = jnp.sum(e, axis=1, keepdims=True)
            level = m + jnp.log(total)
            high = level.astype(BF).astype(F32)
            middle = (level - high).astype(BF).astype(F32)
            side = jnp.where(lane == 0, high, jnp.where(lane == 1, middle, jnp.where(lane == 2, level - high - middle, 0.0)))
            out_ref[part, :cols] = (nn(e.astype(BF), v[start : start + span]) / total).astype(BF)
            out_ref[part, cols:] = side.astype(BF)


def far_kernel(q_hbm, near_hbm, allow_hbm, pack_hbm, _, *rest):
    parts, (out_ref, far_ref, q_ref, near_ref, allow_ref, pack_ref, sem) = rest[:8], rest[8:]
    pairs = [(allow_hbm, allow_ref), (q_hbm, q_ref)] + [(part, far_ref.at[i]) for i, part in enumerate(parts)]
    copies = fetch(pairs + [(near_hbm, near_ref), (pack_hbm, pack_ref)], sem)
    cols = q_ref.shape[1]
    heads = cols // HEAD_DIM
    frames, total_frames = allow_ref.shape
    groups = frames // 4
    chunk = q_ref.shape[0] // groups
    keep = chunk // 4
    rows = chunk * heads
    spread = spreading(keep, heads)
    mine = own_lanes(keep, heads)
    me = lax.axis_index("tm")
    n = lax.broadcasted_iota(jnp.int32, (1, total_frames), 1)
    i, j = (n >> 6) & 3, (n >> 4) & 3
    z = ((me >> 3) - (i ^ (i >> 1))) & 3
    y = ((me >> 1) - (j ^ (j >> 1))) & 3
    where = ((z * 4 + y) * 2 + (me & 1 ^ (n >> 8))) * 16 + (n & 15)
    order = (lax.broadcasted_iota(jnp.int32, (total_frames, total_frames), 0) == where).astype(F32).astype(BF)
    copies[0].wait()
    wall = jnp.where(nn(allow_ref[...].astype(F32).astype(BF), order) > 0.5, 0.0, NEG).astype(BF)
    for copy in copies[1:-1]:
        copy.wait()
    frame = lax.broadcasted_iota(jnp.int32, (rows, frames), 0) // (keep * heads)
    column = lax.broadcasted_iota(jnp.int32, (rows, frames), 1)
    outs = []
    for g in range(groups):
        part = slice(g * rows, (g + 1) * rows)
        q = jnp.where(mine, nn(spread, q_ref[g * chunk : (g + 1) * chunk, :]), 0.0).astype(BF)
        block = nn((column == frame + 4 * g).astype(F32).astype(BF), wall)
        level = jnp.sum(near_ref[part, cols:].astype(F32), axis=1, keepdims=True)
        top = level
        scores = []
        for u in range(4):
            key = far_ref[:, :, u * 16 : (u + 1) * 16, :cols].reshape(total_frames, cols)
            s = nt(q, key) + block
            top = jnp.maximum(top, jnp.max(s, axis=1, keepdims=True))
            scores.append(s)
        total = jnp.exp(level - top)
        acc = total * near_ref[part, :cols].astype(F32)
        for u in range(4):
            e = jnp.exp(scores[u] - top)
            total = total + jnp.sum(e, axis=1, keepdims=True)
            value = far_ref[:, :, u * 16 : (u + 1) * 16, cols:].reshape(total_frames, cols)
            acc = acc + nn(e.astype(BF), value)
        done = jnp.where(mine, acc / total, 0.0).astype(BF)
        outs.append(lax.dot_general(spread, done, (((0,), (0,)), ((), ())), preferred_element_type=F32).astype(BF))
    out = jnp.concatenate(outs, axis=0)
    copies[-1].wait()
    out_ref[...] = nn(pack_ref[...], out).astype(BF).reshape(out_ref.shape)


def final_kernel(*refs):
    sources, (target_ref, loss_ref, att, side, wo, raw, sem) = refs[:16], refs[16:]
    head, core = lax.axis_index("head"), lax.axis_index("tm") & 1
    rows, cols = att.shape[1:]
    half = cols // 2
    width = raw.shape[1]
    here = pl.ds(pl.multiple_of(core * half, 128), half)
    there = pl.ds(pl.multiple_of((1 - core) * half, 128), half)
    targets = [att.at[i] for i in range(4)] + [side.at[i] for i in range(4)]
    targets += [wo.at[i, here] for i in range(4)] + [wo.at[i, there] for i in range(4)]
    for copy in fetch(list(zip(sources, targets)), sem):
        copy.wait()
    raw[...] = sum(nn(att[i], wo[i]) for i in range(4))
    spots = [pl.ds(pl.multiple_of(lax.rem(head + 4 - d, 4) * cols, 128), cols) for d in DISTANCES]
    for i in range(4):
        raw[:, spots[i]] += side[i, :, :cols].astype(F32)
    full = raw[...]
    mean = jnp.sum(full, axis=1, keepdims=True) / width
    var = jnp.sum(full * full, axis=1, keepdims=True) / width - mean * mean
    scale = lax.rsqrt(var + EPS)
    loss = jnp.zeros((rows, 1), F32)
    for i in range(4):
        normed = (raw[:, spots[i]] - mean) * scale
        if i == 0:
            target_ref[...] = normed.astype(BF)
        gap = side[i, :, cols:].astype(F32) - normed
        loss = loss + jnp.sum(gap * gap, axis=1, keepdims=True)
    loss_ref[...] = jnp.broadcast_to(loss / width, (rows, 128)).T[:1]


def whole(n):
    return [pl.BlockSpec(memory_space=pltpu.VMEM) for _ in range(n)]


def params(mib):
    return pltpu.CompilerParams(vmem_limit_bytes=mib * 2**20)


def tm_index(z, y, c):
    return ((z % 4) * 4 + y % 4) * 2 + c


DISTANCES = (0, 1, 3, 2)
PLACES = [(z, y, c) for z in range(4) for y in range(4) for c in range(2)]
FREE = pl.BlockSpec(memory_space=pl.ANY)
HBM = pl.BlockSpec(memory_space=pltpu.HBM)


def along_y(d):
    return [(tm_index(z, y, c), tm_index(z, y + d, c)) for z, y, c in PLACES]


def along_z(d):
    return [(tm_index(z, y, c), tm_index(z + d, y, c)) for z, y, c in PLACES]


OTHER_CORE = [(t, t ^ 1) for t in range(32)]


def body(tokens, w_query, w_key, w_value, w_out, pattern, visible, slot, pred):
    n_peers = lax.axis_size("tm")
    me = lax.axis_index("tm")
    head = lax.axis_index("head")
    n_heads = lax.axis_size("head")
    frames, keep = visible.shape
    width = tokens.shape[1]
    cols = w_query.shape[1]
    own = frames * keep
    steps = frames // 4
    block = 4 * PATCHES
    chunk = 4 * keep
    my_core = me % 2

    r = np.arange(block)
    p = r % PATCHES
    quadrant = 2 * (p // 14 >= 7) + (p % 14 >= 7)
    pool = np.zeros((16, block), np.float32)
    pool[r // PATCHES * 4 + quadrant, r] = 1.0
    n = np.arange(4 * frames)
    order = np.zeros((4 * frames, 4 * frames), np.float32)
    order[n, n % frames * 4 + n // frames] = 1.0

    mine, q, tok = pl.pallas_call(
        gather_kernel,
        in_specs=[HBM] * 4 + whole(3),
        out_specs=whole(3),
        out_shape=[
            jax.ShapeDtypeStruct((4 * frames, 2 * cols), BF),
            jax.ShapeDtypeStruct((own, cols), BF),
            jax.ShapeDtypeStruct((own, cols), BF),
        ],
        scratch_shapes=[pltpu.VMEM((frames * PATCHES, width), BF)]
        + [pltpu.VMEM((width, cols), BF)] * 3
        + [pltpu.VMEM((4 * frames, width), F32), pltpu.VMEM((own, width), BF), pltpu.SemaphoreType.DMA((steps + 3,))],
        compiler_params=params(60),
        cost_estimate=pl.CostEstimate(flops=2 * 10**9, bytes_accessed=10**7, transcendentals=0),
        name="gather",
    )(tokens, w_query, w_key, w_value, jnp.asarray(pool, BF), visible, jnp.asarray(order, BF))

    plane = jnp.stack([mine] + [lax.ppermute(mine, "tm", along_y(d)) for d in DISTANCES[1:]])
    plane, q, tok = lax.optimization_barrier((plane, q, tok))
    parts = [plane] + [lax.ppermute(plane, "tm", along_z(d)) for d in DISTANCES[1:]]
    owner_all = slot // own
    my_slots = lax.dynamic_slice_in_dim(slot, me * own, own)
    my_owner = my_slots // own
    before = np.tril(np.ones((own, own), np.float32), -1)
    same = (my_owner[:, None] == my_owner[None, :]) & (before > 0)
    place = my_owner * CAP + jnp.sum(same, axis=1, dtype=jnp.int32)
    pack = (jnp.arange(n_peers * CAP, dtype=jnp.int32)[:, None] == place[None, :]).astype(BF)
    coming = (owner_all == me).reshape(n_peers, own)
    rank = jnp.dot(coming.astype(BF), jnp.asarray(before.T, BF), preferred_element_type=F32).astype(jnp.int32)
    rank = jnp.where(coming, rank, -1)
    hit = rank[:, None, :] == jnp.arange(CAP, dtype=jnp.int32)[None, :, None]
    student = jnp.max(jnp.where(hit, (slot % own).reshape(n_peers, 1, own), -1), axis=2)
    unpack = (jnp.arange(own, dtype=jnp.int32)[:, None] == student.reshape(1, -1)).astype(BF)

    def deliver(packed):
        return lax.all_to_all(packed, "tm", 0, 0, tiled=True)

    def arrange(got):
        return jnp.dot(unpack, got.reshape(n_peers * CAP, -1), preferred_element_type=F32).astype(BF)

    tok_got = deliver(jnp.dot(pack, tok, preferred_element_type=F32).astype(BF).reshape(n_peers, CAP, cols))

    heads = cols // HEAD_DIM
    near = pl.pallas_call(
        near_kernel,
        in_specs=[HBM] * 4,
        out_specs=pl.BlockSpec(memory_space=pltpu.VMEM),
        out_shape=jax.ShapeDtypeStruct((own * heads, cols + 128), BF),
        scratch_shapes=[pltpu.VMEM((own, cols), BF), pltpu.VMEM((frames * PATCHES, width), BF)]
        + [pltpu.VMEM((width, cols), BF)] * 2
        + [pltpu.SemaphoreType.DMA((steps + 3,))],
        compiler_params=params(60),
        cost_estimate=pl.CostEstimate(flops=5 * 10**9, bytes_accessed=10**7, transcendentals=10**6),
        name="near",
    )(q, tokens, w_key, w_value)

    plane, near = lax.optimization_barrier((plane, near))
    parts = parts + [lax.ppermute(part, "tm", OTHER_CORE) for part in [plane] + parts[1:]]
    packed = pl.pallas_call(
        far_kernel,
        in_specs=[HBM] * 13,
        out_specs=pl.BlockSpec(memory_space=pltpu.VMEM),
        out_shape=jax.ShapeDtypeStruct((n_peers, CAP, cols), BF),
        scratch_shapes=[
            pltpu.VMEM((8, 4, 4 * frames, 2 * cols), BF),
            pltpu.VMEM((own, cols), BF),
            pltpu.VMEM((own * heads, cols + 128), BF),
            pltpu.VMEM(pattern.shape, jnp.int32),
            pltpu.VMEM(pack.shape, BF),
            pltpu.SemaphoreType.DMA((12,)),
        ],
        compiler_params=params(60),
        cost_estimate=pl.CostEstimate(flops=4 * 10**9, bytes_accessed=4 * 10**6, transcendentals=3 * 10**6),
        name="far",
    )(q, near, pattern, pack, tok_got, *parts)
    tok_own = arrange(tok_got)
    att = arrange(deliver(packed))

    def to(d):
        return [(h, (h + d) % n_heads) for h in range(n_heads)]

    def over_heads(x):
        return [x] + [lax.ppermute(x, "head", to(d)) for d in DISTANCES[1:]]

    half = cols // 2
    halves = over_heads(lax.dynamic_slice_in_dim(w_out, my_core * half, half, 0))
    other = [lax.ppermute(piece, "tm", OTHER_CORE) for piece in halves]
    side = over_heads(jnp.concatenate([tok_own, pred], axis=1))

    target, row_loss = pl.pallas_call(
        final_kernel,
        in_specs=[HBM] * 16,
        out_specs=whole(2),
        out_shape=[jax.ShapeDtypeStruct((own, cols), BF), jax.ShapeDtypeStruct((1, own), F32)],
        scratch_shapes=[
            pltpu.VMEM((4, own, cols), BF),
            pltpu.VMEM((4, own, 2 * cols), BF),
            pltpu.VMEM((4, cols, width), BF),
            pltpu.VMEM((own, width), F32),
            pltpu.SemaphoreType.DMA((16,)),
        ],
        compiler_params=params(16),
        cost_estimate=pl.CostEstimate(flops=10**9, bytes_accessed=4 * 10**6, transcendentals=0),
        name="final",
    )(*over_heads(att), *side, *halves, *other)
    return target, row_loss.reshape(own)


def solution(mesh):
    return jax.shard_map(
        body,
        mesh=mesh,
        in_specs=(
            P("tm", None),
            P(None, "head"),
            P(None, "head"),
            P(None, "head"),
            P("head", None),
            P("tm", None),
            P("tm", None),
            P(),
            P("tm", "head"),
        ),
        out_specs=(P("tm", "head"), P("tm")),
        check_vma=False,
    )
```

```python
import numpy as np

import jax
import jax.numpy as jnp
from jax import lax
from jax.experimental import pallas as pl
from jax.experimental.pallas import tpu as pltpu
from jax.sharding import PartitionSpec as P

HEAD_DIM = 64
PATCHES = 196
CAP = 48
NEG = -1e30
EPS = 1e-06
BF = jnp.bfloat16
F32 = jnp.float32


def nt(a, b):
    return lax.dot_general(a, b, (((1,), (1,)), ((), ())), preferred_element_type=F32)


def nn(a, b):
    return lax.dot_general(a, b, (((1,), (0,)), ((), ())), preferred_element_type=F32)


def fetch(pairs, sem):
    copies = [pltpu.make_async_copy(source, target, sem.at[i]) for i, (source, target) in enumerate(pairs)]
    for copy in copies:
        copy.start()
    return copies


def row_blocks(ref, count):
    size = ref.shape[0] // count
    return [ref.at[pl.ds(i * size, size)] for i in range(count)]


def gather_kernel(
    x_hbm, wq_hbm, wk_hbm, wv_hbm, pool_ref, vis_ref, order_ref, chunk_ref, q_ref, t_ref, x_ref, wq_ref, wk_ref, wv_ref, sums, rows_in, sem
):
    steps = vis_ref.shape[0] // 4
    pairs = list(zip(row_blocks(x_hbm, steps), row_blocks(x_ref, steps)))
    copies = fetch(pairs + [(wk_hbm, wk_ref), (wv_hbm, wv_ref), (wq_hbm, wq_ref)], sem)
    rows = x_ref.shape[0] // steps
    frames, keep = vis_ref.shape
    count = 4 * keep
    cols = wk_ref.shape[1]
    r = lax.broadcasted_iota(jnp.int32, (count, 1), 0)
    frame = sum((r >= keep * i).astype(jnp.int32) for i in (1, 2, 3))
    spot = lax.broadcasted_iota(jnp.int32, (count, keep), 1) == r - keep * frame
    for step in range(steps):
        mine = (lax.broadcasted_iota(jnp.int32, (count, frames), 1) == frame + step * 4).astype(F32).astype(BF)
        seen = nn(mine, vis_ref[...].astype(F32).astype(BF))
        pos = jnp.sum(jnp.where(spot, seen, 0.0), axis=1, keepdims=True).astype(jnp.int32) + frame * PATCHES
        pick = (pos == lax.broadcasted_iota(jnp.int32, (count, rows), 1)).astype(F32).astype(BF)
        choose = jnp.concatenate([pool_ref[...], pick], axis=0)
        copies[step].wait()
        both = nn(choose, x_ref[step * rows : (step + 1) * rows, :])
        sums[step * 16 : (step + 1) * 16, :] = both[:16]
        rows_in[step * count : (step + 1) * count, :] = both[16:].astype(BF)
    total = sums[...]
    count = total.shape[0]
    high = total.astype(BF)
    low = (total - high.astype(F32)).astype(BF)
    pair = jnp.concatenate([high, low], axis=0)
    order = order_ref[...]
    for i, w_ref in enumerate((wk_ref, wv_ref)):
        copies[steps + i].wait()
        field = nn(pair, w_ref[...])
        pooled = ((field[:count] + field[count:]) / 7.0).astype(BF)
        chunk_ref[:, i * cols : (i + 1) * cols] = nn(order, pooled).astype(BF)
    copies[steps + 2].wait()
    q = nn(rows_in[...], wq_ref[...]).astype(BF).astype(F32) * HEAD_DIM ** -0.5
    q_ref[...] = q.astype(BF)
    t_ref[q_ref.shape[0] :, :] = jnp.zeros((t_ref.shape[0] - q_ref.shape[0], cols), BF)
    t_ref[: q_ref.shape[0], :] = rows_in[:, pl.ds(pl.multiple_of(lax.axis_index("head") * cols, 128), cols)]


def row_order(keep, heads):
    rows, chunk, cols = 4 * keep * heads, 4 * keep, heads * HEAD_DIM

    def split(r):
        frame = sum((r >= keep * heads * i).astype(jnp.int32) for i in (1, 2, 3))
        r = r - frame * keep * heads
        head = sum((r >= keep * i).astype(jnp.int32) for i in range(1, heads))
        return frame * keep + r - head * keep, head

    source, head = split(lax.broadcasted_iota(jnp.int32, (rows, 1), 0))
    spread = (source == lax.broadcasted_iota(jnp.int32, (rows, chunk), 1)).astype(F32).astype(BF)
    lanes = (head == lax.broadcasted_iota(jnp.int32, (rows, cols), 1) >> 6).astype(F32).astype(BF)
    source, _ = split(lax.broadcasted_iota(jnp.int32, (1, rows), 1))
    join = (source == lax.broadcasted_iota(jnp.int32, (chunk, rows), 0)).astype(F32).astype(BF)
    return spread, lanes, join


def near_kernel(q_hbm, x_hbm, wk_hbm, wv_hbm, out_ref, q_ref, x_ref, wk_ref, wv_ref, sem):
    heads = wk_ref.shape[1] // HEAD_DIM
    steps = x_ref.shape[0] // (4 * PATCHES)
    chunk = q_ref.shape[0] // steps
    pairs = list(zip(row_blocks(x_hbm, steps), row_blocks(x_ref, steps)))
    copies = fetch([(wk_hbm, wk_ref)] + pairs[:1] + [(wv_hbm, wv_ref), (q_hbm, q_ref)] + pairs[1:], sem)
    size = x_ref.shape[0] // steps
    cols = q_ref.shape[1]
    rows = chunk // 4 * heads
    span = 208
    starts = [f * PATCHES // 16 * 16 for f in range(4)]
    c = lax.broadcasted_iota(jnp.int32, (rows, span), 1)
    walls = [jnp.where((c >= f * PATCHES - starts[f]) & (c < (f + 1) * PATCHES - starts[f]), 0.0, NEG) for f in range(4)]
    lane = lax.broadcasted_iota(jnp.int32, (4 * rows, 128), 1)
    spread, lanes, _ = row_order(chunk // 4, heads)
    for copy in copies[:4]:
        copy.wait()
    for step in range(steps):
        if step:
            copies[3 + step].wait()
        x = x_ref[step * size : (step + 1) * size, :]
        k = nn(x, wk_ref[...]).astype(BF)
        v = nn(x, wv_ref[...]).astype(BF)
        stack = nn(spread, q_ref[step * chunk : (step + 1) * chunk, :]).astype(BF) * lanes
        s = jnp.concatenate(
            [nt(stack[f * rows : (f + 1) * rows], k[starts[f] : starts[f] + span]) + walls[f] for f in range(4)], axis=0
        )
        m = jnp.max(s, axis=1, keepdims=True)
        e = jnp.exp(s - m)
        total = jnp.sum(e, axis=1, keepdims=True)
        e = e.astype(BF)
        o = jnp.concatenate(
            [nn(e[f * rows : (f + 1) * rows], v[starts[f] : starts[f] + span]) for f in range(4)], axis=0
        )
        level = m + jnp.log(total)
        high = level.astype(BF).astype(F32)
        middle = (level - high).astype(BF).astype(F32)
        side = jnp.where(lane == 0, high, jnp.where(lane == 1, middle, jnp.where(lane == 2, level - high - middle, 0.0)))
        part = slice(step * 4 * rows, (step + 1) * 4 * rows)
        out_ref[part, :cols] = (o * (1.0 / total)).astype(BF)
        out_ref[part, cols:] = side.astype(BF)


def far_kernel(q_hbm, near_hbm, allow_hbm, pack_hbm, _, *rest):
    parts, rest = rest[:8], rest[8:]
    out_ref, far_ref, key, value, q_ref, near_ref, allow_ref, pack_ref, sem = rest
    pairs = [(allow_hbm, allow_ref)] + [(part, far_ref.at[i]) for i, part in enumerate(parts)]
    copies = fetch(pairs + [(q_hbm, q_ref), (near_hbm, near_ref), (pack_hbm, pack_ref)], sem)
    cols = q_ref.shape[1]
    frames, total_frames = allow_ref.shape
    groups = frames // 4
    chunk = q_ref.shape[0] // groups
    keep = chunk // 4
    heads = cols // HEAD_DIM
    rows = chunk * heads
    spread, lanes, join = row_order(keep, heads)
    column = lax.broadcasted_iota(jnp.int32, (rows, frames), 1)
    r = lax.broadcasted_iota(jnp.int32, (rows, frames), 0)
    frame = sum((r >= keep * heads * i).astype(jnp.int32) for i in (1, 2, 3))
    me = lax.axis_index("tm")
    n = lax.broadcasted_iota(jnp.int32, (1, total_frames), 1)
    i, j = (n >> 6) & 3, (n >> 4) & 3
    z = ((me >> 3) - (i ^ (i >> 1))) & 3
    y = ((me >> 1) - (j ^ (j >> 1))) & 3
    where = ((z * 4 + y) * 2 + (me & 1 ^ (n >> 8))) * 16 + (n & 15)
    order = (lax.broadcasted_iota(jnp.int32, (total_frames, total_frames), 0) == where).astype(F32).astype(BF)
    copies[0].wait()
    wall = jnp.where(nn(allow_ref[...].astype(F32).astype(BF), order) > 0.5, 0.0, NEG).astype(BF)
    for p in range(8):
        copies[1 + p].wait()
        spot = slice(p * 64, (p + 1) * 64)
        for u in range(4):
            key[u, spot, :] = far_ref[p, :, u * 16 : (u + 1) * 16, :cols].reshape(64, cols)
            value[u, spot, :] = far_ref[p, :, u * 16 : (u + 1) * 16, cols:].reshape(64, cols)
    copies[9].wait()
    copies[10].wait()
    outs = []
    for g in range(groups):
        part = slice(g * rows, (g + 1) * rows)
        q = nn(spread, q_ref[g * chunk : (g + 1) * chunk, :]).astype(BF) * lanes
        block = nn((column == frame + 4 * g).astype(F32).astype(BF), wall)
        level = jnp.sum(near_ref[part, cols:].astype(F32), axis=1, keepdims=True)
        top = level
        scores = []
        for u in range(4):
            s = nt(q, key[u]) + block
            top = jnp.maximum(top, jnp.max(s, axis=1, keepdims=True))
            scores.append(s)
        total = jnp.exp(level - top)
        acc = total * near_ref[part, :cols].astype(F32)
        for u in range(4):
            e = jnp.exp(scores[u] - top)
            total = total + jnp.sum(e, axis=1, keepdims=True)
            acc = acc + nn(e.astype(BF), value[u])
        outs.append((acc * (1.0 / total)).astype(BF) * lanes)
    outs = [nn(join, done).astype(BF) for done in outs]
    outs.append(jnp.zeros((pack_ref.shape[1] - chunk * groups, cols), BF))
    out = jnp.concatenate(outs, axis=0)
    copies[11].wait()
    out_ref[...] = nn(pack_ref[...], out).astype(BF).reshape(out_ref.shape)


def final_kernel(*refs):
    sources, (target_ref, loss_ref, att, side, wo, raw, sem) = refs[:16], refs[16:]
    head, core = lax.axis_index("head"), lax.axis_index("tm") & 1
    rows, cols = att.shape[1:]
    half = cols // 2
    width = raw.shape[1]
    here = pl.ds(pl.multiple_of(core * half, 128), half)
    there = pl.ds(pl.multiple_of((1 - core) * half, 128), half)
    targets = [att.at[i] for i in range(4)] + [side.at[i] for i in range(4)]
    targets += [wo.at[i, here] for i in range(4)] + [wo.at[i, there] for i in range(4)]
    copies = fetch(list(zip(sources, targets)), sem)
    for copy in copies[:4] + copies[8:]:
        copy.wait()
    raw[...] = sum(nn(att[i], wo[i]) for i in range(4))
    spots = [pl.ds(pl.multiple_of(lax.rem(head + 4 - d, 4) * cols, 128), cols) for d in DISTANCES]
    for copy in copies[4:8]:
        copy.wait()
    for i in range(4):
        raw[:, spots[i]] += side[i, :, :cols].astype(F32)
    full = raw[...]
    mean = jnp.sum(full, axis=1, keepdims=True) / width
    var = jnp.sum(full * full, axis=1, keepdims=True) / width - mean * mean
    scale = lax.rsqrt(var + EPS)
    loss = jnp.zeros((rows, 1), F32)
    for i in range(4):
        normed = (raw[:, spots[i]] - mean) * scale
        if i == 0:
            target_ref[...] = normed.astype(BF)
        gap = side[i, :, cols:].astype(F32) - normed
        loss = loss + jnp.sum(gap * gap, axis=1, keepdims=True)
    loss_ref[...] = jnp.broadcast_to(loss / width, (rows, 128)).T[:1]


def whole(n):
    return [pl.BlockSpec(memory_space=pltpu.VMEM) for _ in range(n)]


def params(mib):
    return pltpu.CompilerParams(vmem_limit_bytes=mib * 2**20)


def tm_index(z, y, c):
    return ((z % 4) * 4 + y % 4) * 2 + c


DISTANCES = (0, 1, 3, 2)
PLACES = [(z, y, c) for z in range(4) for y in range(4) for c in range(2)]
FREE = pl.BlockSpec(memory_space=pl.ANY)
HBM = pl.BlockSpec(memory_space=pltpu.HBM)


def along_y(d):
    return [(tm_index(z, y, c), tm_index(z, y + d, c)) for z, y, c in PLACES]


def along_z(d):
    return [(tm_index(z, y, c), tm_index(z + d, y, c)) for z, y, c in PLACES]


OTHER_CORE = [(t, t ^ 1) for t in range(32)]


def body(tokens, w_query, w_key, w_value, w_out, pattern, visible, slot, pred):
    n_peers = lax.axis_size("tm")
    me = lax.axis_index("tm")
    head = lax.axis_index("head")
    n_heads = lax.axis_size("head")
    frames, keep = visible.shape
    width = tokens.shape[1]
    cols = w_query.shape[1]
    own = frames * keep
    steps = frames // 4
    block = 4 * PATCHES
    chunk = 4 * keep
    padded = -(-own // 128) * 128
    my_core = me % 2

    r = np.arange(block)
    p = r % PATCHES
    quadrant = 2 * (p // 14 >= 7) + (p % 14 >= 7)
    pool = np.zeros((16, block), np.float32)
    pool[r // PATCHES * 4 + quadrant, r] = 1.0
    n = np.arange(4 * frames)
    order = np.zeros((4 * frames, 4 * frames), np.float32)
    order[n, n % frames * 4 + n // frames] = 1.0

    mine, q, tok = pl.pallas_call(
        gather_kernel,
        in_specs=[HBM] * 4 + whole(3),
        out_specs=whole(3),
        out_shape=[
            jax.ShapeDtypeStruct((4 * frames, 2 * cols), BF),
            jax.ShapeDtypeStruct((own, cols), BF),
            jax.ShapeDtypeStruct((padded, cols), BF),
        ],
        scratch_shapes=[pltpu.VMEM((frames * PATCHES, width), BF)]
        + [pltpu.VMEM((width, cols), BF)] * 3
        + [pltpu.VMEM((4 * frames, width), F32), pltpu.VMEM((own, width), BF), pltpu.SemaphoreType.DMA((steps + 3,))],
        compiler_params=params(60),
        cost_estimate=pl.CostEstimate(flops=2 * 10**9, bytes_accessed=10**7, transcendentals=0),
        name="gather",
    )(tokens, w_query, w_key, w_value, jnp.asarray(pool, BF), visible, jnp.asarray(order, BF))

    plane = jnp.stack([mine] + [lax.ppermute(mine, "tm", along_y(d)) for d in DISTANCES[1:]])
    plane, q, tok = lax.optimization_barrier((plane, q, tok))
    parts = [plane] + [lax.ppermute(plane, "tm", along_z(d)) for d in DISTANCES[1:]]
    owner_all = slot // own
    my_slots = lax.dynamic_slice_in_dim(slot, me * own, own)
    my_owner = my_slots // own
    before = np.tril(np.ones((own, own), np.float32), -1)
    same = (my_owner[:, None] == my_owner[None, :]) & (before > 0)
    place = my_owner * CAP + jnp.sum(same, axis=1, dtype=jnp.int32)
    place = jnp.pad(place, (0, padded - own), constant_values=-1)
    pack = (jnp.arange(n_peers * CAP, dtype=jnp.int32)[:, None] == place[None, :]).astype(BF)
    coming = (owner_all == me).reshape(n_peers, own)
    rank = jnp.dot(coming.astype(BF), jnp.asarray(before.T, BF), preferred_element_type=F32).astype(jnp.int32)
    rank = jnp.where(coming, rank, -1)
    hit = rank[:, None, :] == jnp.arange(CAP, dtype=jnp.int32)[None, :, None]
    student = jnp.max(jnp.where(hit, (slot % own).reshape(n_peers, 1, own), -1), axis=2)
    unpack = (jnp.arange(own, dtype=jnp.int32)[:, None] == student.reshape(1, -1)).astype(BF)

    def deliver(packed):
        return lax.all_to_all(packed, "tm", 0, 0, tiled=True)

    def arrange(got):
        return jnp.dot(unpack, got.reshape(n_peers * CAP, -1), preferred_element_type=F32).astype(BF)

    tok_got = deliver(jnp.dot(pack, tok, preferred_element_type=F32).astype(BF).reshape(n_peers, CAP, cols))

    heads = cols // HEAD_DIM
    near = pl.pallas_call(
        near_kernel,
        in_specs=[HBM] * 4,
        out_specs=pl.BlockSpec(memory_space=pltpu.VMEM),
        out_shape=jax.ShapeDtypeStruct((own * heads, cols + 128), BF),
        scratch_shapes=[pltpu.VMEM((own, cols), BF), pltpu.VMEM((frames * PATCHES, width), BF)]
        + [pltpu.VMEM((width, cols), BF)] * 2
        + [pltpu.SemaphoreType.DMA((steps + 3,))],
        compiler_params=params(60),
        cost_estimate=pl.CostEstimate(flops=5 * 10**9, bytes_accessed=10**7, transcendentals=10**6),
        name="near",
    )(q, tokens, w_key, w_value)

    plane, near = lax.optimization_barrier((plane, near))
    parts = parts + [lax.ppermute(part, "tm", OTHER_CORE) for part in [plane] + parts[1:]]
    packed = pl.pallas_call(
        far_kernel,
        in_specs=[HBM] * 13,
        out_specs=pl.BlockSpec(memory_space=pltpu.VMEM),
        out_shape=jax.ShapeDtypeStruct((n_peers, CAP, cols), BF),
        scratch_shapes=[
            pltpu.VMEM((8, 4, 4 * frames, 2 * cols), BF),
            pltpu.VMEM((4, n_peers * frames, cols), BF),
            pltpu.VMEM((4, n_peers * frames, cols), BF),
            pltpu.VMEM((own, cols), BF),
            pltpu.VMEM((own * heads, cols + 128), BF),
            pltpu.VMEM(pattern.shape, jnp.int32),
            pltpu.VMEM(pack.shape, BF),
            pltpu.SemaphoreType.DMA((12,)),
        ],
        compiler_params=params(60),
        cost_estimate=pl.CostEstimate(flops=4 * 10**9, bytes_accessed=4 * 10**6, transcendentals=3 * 10**6),
        name="far",
    )(q, near, pattern, pack, tok_got, *parts)
    tok_own = arrange(tok_got)
    att = arrange(deliver(packed))

    def to(d):
        return [(h, (h + d) % n_heads) for h in range(n_heads)]

    def over_heads(x):
        return [x] + [lax.ppermute(x, "head", to(d)) for d in DISTANCES[1:]]

    half = cols // 2
    halves = over_heads(lax.dynamic_slice_in_dim(w_out, my_core * half, half, 0))
    other = [lax.ppermute(piece, "tm", OTHER_CORE) for piece in halves]
    side = over_heads(jnp.concatenate([tok_own, pred], axis=1))

    target, row_loss = pl.pallas_call(
        final_kernel,
        in_specs=[HBM] * 16,
        out_specs=whole(2),
        out_shape=[jax.ShapeDtypeStruct((own, cols), BF), jax.ShapeDtypeStruct((1, own), F32)],
        scratch_shapes=[
            pltpu.VMEM((4, own, cols), BF),
            pltpu.VMEM((4, own, 2 * cols), BF),
            pltpu.VMEM((4, cols, width), BF),
            pltpu.VMEM((own, width), F32),
            pltpu.SemaphoreType.DMA((16,)),
        ],
        compiler_params=params(16),
        cost_estimate=pl.CostEstimate(flops=10**9, bytes_accessed=4 * 10**6, transcendentals=0),
        name="final",
    )(*over_heads(att), *side, *halves, *other)
    return target, row_loss.reshape(own)


def solution(mesh):
    return jax.shard_map(
        body,
        mesh=mesh,
        in_specs=(
            P("tm", None),
            P(None, "head"),
            P(None, "head"),
            P(None, "head"),
            P("head", None),
            P("tm", None),
            P("tm", None),
            P(),
            P("tm", "head"),
        ),
        out_specs=(P("tm", "head"), P("tm")),
        check_vma=False,
    )
```

```python
import numpy as np

import jax
import jax.numpy as jnp
from jax import lax
from jax.experimental import pallas as pl
from jax.experimental.pallas import tpu as pltpu
from jax.sharding import PartitionSpec as P

HEAD_DIM = 64
PATCHES = 196
CAP = 48
NEG = -1e30
EPS = 1e-06
BF = jnp.bfloat16
F32 = jnp.float32


def nt(a, b):
    return lax.dot_general(a, b, (((1,), (1,)), ((), ())), preferred_element_type=F32)


def nn(a, b):
    return lax.dot_general(a, b, (((1,), (0,)), ((), ())), preferred_element_type=F32)


def fetch(pairs, sem):
    copies = [pltpu.make_async_copy(source, target, sem.at[i]) for i, (source, target) in enumerate(pairs)]
    for copy in copies:
        copy.start()
    return copies


def row_blocks(ref, count):
    size = ref.shape[0] // count
    return [ref.at[pl.ds(i * size, size)] for i in range(count)]


def gather_kernel(
    x_hbm, wq_hbm, wk_hbm, wv_hbm, pool_ref, vis_ref, order_ref, chunk_ref, q_ref, t_ref, x_ref, wq_ref, wk_ref, wv_ref, sums, rows_in, sem
):
    steps = vis_ref.shape[0] // 4
    pairs = list(zip(row_blocks(x_hbm, steps), row_blocks(x_ref, steps)))
    copies = fetch(pairs + [(wk_hbm, wk_ref), (wv_hbm, wv_ref), (wq_hbm, wq_ref)], sem)
    rows = x_ref.shape[0] // steps
    frames, keep = vis_ref.shape
    count = 4 * keep
    cols = wk_ref.shape[1]
    r = lax.broadcasted_iota(jnp.int32, (count, 1), 0)
    frame = sum((r >= keep * i).astype(jnp.int32) for i in (1, 2, 3))
    spot = lax.broadcasted_iota(jnp.int32, (count, keep), 1) == r - keep * frame
    for step in range(steps):
        mine = (lax.broadcasted_iota(jnp.int32, (count, frames), 1) == frame + step * 4).astype(F32).astype(BF)
        seen = nn(mine, vis_ref[...].astype(F32).astype(BF))
        pos = jnp.sum(jnp.where(spot, seen, 0.0), axis=1, keepdims=True).astype(jnp.int32) + frame * PATCHES
        pick = (pos == lax.broadcasted_iota(jnp.int32, (count, rows), 1)).astype(F32).astype(BF)
        choose = jnp.concatenate([pool_ref[...], pick], axis=0)
        copies[step].wait()
        both = nn(choose, x_ref[step * rows : (step + 1) * rows, :])
        sums[step * 16 : (step + 1) * 16, :] = both[:16]
        rows_in[step * count : (step + 1) * count, :] = both[16:].astype(BF)
    total = sums[...]
    count = total.shape[0]
    high = total.astype(BF)
    low = (total - high.astype(F32)).astype(BF)
    pair = jnp.concatenate([high, low], axis=0)
    order = order_ref[...]
    for i, w_ref in enumerate((wk_ref, wv_ref)):
        copies[steps + i].wait()
        field = nn(pair, w_ref[...])
        pooled = ((field[:count] + field[count:]) / 7.0).astype(BF)
        chunk_ref[:, i * cols : (i + 1) * cols] = nn(order, pooled).astype(BF)
    copies[steps + 2].wait()
    q = nn(rows_in[...], wq_ref[...]).astype(BF).astype(F32) * HEAD_DIM ** -0.5
    q_ref[...] = q.astype(BF)
    t_ref[q_ref.shape[0] :, :] = jnp.zeros((t_ref.shape[0] - q_ref.shape[0], cols), BF)
    t_ref[: q_ref.shape[0], :] = rows_in[:, pl.ds(pl.multiple_of(lax.axis_index("head") * cols, 128), cols)]


def row_order(keep, heads):
    rows, chunk, cols = 4 * keep * heads, 4 * keep, heads * HEAD_DIM

    def split(r):
        frame = sum((r >= keep * heads * i).astype(jnp.int32) for i in (1, 2, 3))
        r = r - frame * keep * heads
        head = sum((r >= keep * i).astype(jnp.int32) for i in range(1, heads))
        return frame * keep + r - head * keep, head

    source, head = split(lax.broadcasted_iota(jnp.int32, (rows, 1), 0))
    spread = (source == lax.broadcasted_iota(jnp.int32, (rows, chunk), 1)).astype(F32).astype(BF)
    lanes = (head == lax.broadcasted_iota(jnp.int32, (rows, cols), 1) >> 6).astype(F32).astype(BF)
    source, _ = split(lax.broadcasted_iota(jnp.int32, (1, rows), 1))
    join = (source == lax.broadcasted_iota(jnp.int32, (chunk, rows), 0)).astype(F32).astype(BF)
    return spread, lanes, join


def near_kernel(q_hbm, x_hbm, wk_hbm, wv_hbm, out_ref, q_ref, x_ref, wk_ref, wv_ref, sem):
    heads = wk_ref.shape[1] // HEAD_DIM
    steps = x_ref.shape[0] // (4 * PATCHES)
    chunk = q_ref.shape[0] // steps
    pairs = list(zip(row_blocks(x_hbm, steps), row_blocks(x_ref, steps)))
    copies = fetch([(wk_hbm, wk_ref)] + pairs[:1] + [(wv_hbm, wv_ref), (q_hbm, q_ref)] + pairs[1:], sem)
    size = x_ref.shape[0] // steps
    cols = q_ref.shape[1]
    rows = chunk // 4 * heads
    span = 208
    starts = [f * PATCHES // 16 * 16 for f in range(4)]
    c = lax.broadcasted_iota(jnp.int32, (rows, span), 1)
    walls = [jnp.where((c >= f * PATCHES - starts[f]) & (c < (f + 1) * PATCHES - starts[f]), 0.0, NEG) for f in range(4)]
    lane = lax.broadcasted_iota(jnp.int32, (4 * rows, 128), 1)
    spread, lanes, _ = row_order(chunk // 4, heads)
    for copy in copies[:4]:
        copy.wait()
    for step in range(steps):
        if step:
            copies[3 + step].wait()
        x = x_ref[step * size : (step + 1) * size, :]
        k = nn(x, wk_ref[...]).astype(BF)
        v = nn(x, wv_ref[...]).astype(BF)
        stack = nn(spread, q_ref[step * chunk : (step + 1) * chunk, :]).astype(BF) * lanes
        s = jnp.concatenate(
            [nt(stack[f * rows : (f + 1) * rows], k[starts[f] : starts[f] + span]) + walls[f] for f in range(4)], axis=0
        )
        m = jnp.max(s, axis=1, keepdims=True)
        e = jnp.exp(s - m)
        total = jnp.sum(e, axis=1, keepdims=True)
        e = e.astype(BF)
        o = jnp.concatenate(
            [nn(e[f * rows : (f + 1) * rows], v[starts[f] : starts[f] + span]) for f in range(4)], axis=0
        )
        level = m + jnp.log(total)
        high = level.astype(BF).astype(F32)
        middle = (level - high).astype(BF).astype(F32)
        side = jnp.where(lane == 0, high, jnp.where(lane == 1, middle, jnp.where(lane == 2, level - high - middle, 0.0)))
        part = slice(step * 4 * rows, (step + 1) * 4 * rows)
        out_ref[part, :cols] = (o * (1.0 / total)).astype(BF)
        out_ref[part, cols:] = side.astype(BF)


def far_kernel(q_hbm, near_hbm, allow_hbm, pack_hbm, _, *rest):
    parts, rest = rest[:8], rest[8:]
    out_ref, far_ref, key, value, q_ref, near_ref, allow_ref, pack_ref, sem = rest
    pairs = [(allow_hbm, allow_ref)] + [(part, far_ref.at[i]) for i, part in enumerate(parts)]
    copies = fetch(pairs + [(q_hbm, q_ref), (near_hbm, near_ref), (pack_hbm, pack_ref)], sem)
    cols = q_ref.shape[1]
    frames, total_frames = allow_ref.shape
    groups = frames // 4
    chunk = q_ref.shape[0] // groups
    keep = chunk // 4
    heads = cols // HEAD_DIM
    rows = chunk * heads
    spread, lanes, join = row_order(keep, heads)
    column = lax.broadcasted_iota(jnp.int32, (rows, frames), 1)
    r = lax.broadcasted_iota(jnp.int32, (rows, frames), 0)
    frame = sum((r >= keep * heads * i).astype(jnp.int32) for i in (1, 2, 3))
    me = lax.axis_index("tm")
    n = lax.broadcasted_iota(jnp.int32, (1, total_frames), 1)
    i, j = (n >> 6) & 3, (n >> 4) & 3
    z = ((me >> 3) - (i ^ (i >> 1))) & 3
    y = ((me >> 1) - (j ^ (j >> 1))) & 3
    where = ((z * 4 + y) * 2 + (me & 1 ^ (n >> 8))) * 16 + (n & 15)
    order = (lax.broadcasted_iota(jnp.int32, (total_frames, total_frames), 0) == where).astype(F32).astype(BF)
    copies[0].wait()
    wall = jnp.where(nn(allow_ref[...].astype(F32).astype(BF), order) > 0.5, 0.0, NEG).astype(BF)
    for p in range(8):
        copies[1 + p].wait()
        spot = slice(p * 64, (p + 1) * 64)
        for u in range(4):
            key[u, spot, :] = far_ref[p, :, u * 16 : (u + 1) * 16, :cols].reshape(64, cols)
            value[u, spot, :] = far_ref[p, :, u * 16 : (u + 1) * 16, cols:].reshape(64, cols)
    copies[9].wait()
    copies[10].wait()
    outs = []
    for g in range(groups):
        part = slice(g * rows, (g + 1) * rows)
        q = nn(spread, q_ref[g * chunk : (g + 1) * chunk, :]).astype(BF) * lanes
        block = nn((column == frame + 4 * g).astype(F32).astype(BF), wall)
        level = jnp.sum(near_ref[part, cols:].astype(F32), axis=1, keepdims=True)
        top = level
        scores = []
        for u in range(4):
            s = nt(q, key[u]) + block
            top = jnp.maximum(top, jnp.max(s, axis=1, keepdims=True))
            scores.append(s)
        total = jnp.exp(level - top)
        acc = total * near_ref[part, :cols].astype(F32)
        for u in range(4):
            e = jnp.exp(scores[u] - top)
            total = total + jnp.sum(e, axis=1, keepdims=True)
            acc = acc + nn(e.astype(BF), value[u])
        outs.append((acc * (1.0 / total)).astype(BF) * lanes)
    outs = [nn(join, done).astype(BF) for done in outs]
    outs.append(jnp.zeros((pack_ref.shape[1] - chunk * groups, cols), BF))
    out = jnp.concatenate(outs, axis=0)
    copies[11].wait()
    out_ref[...] = nn(pack_ref[...], out).astype(BF).reshape(out_ref.shape)


def final_kernel(*refs):
    sources, (target_ref, loss_ref, att, side, wo, raw, sem) = refs[:16], refs[16:]
    head, core = lax.axis_index("head"), lax.axis_index("tm") & 1
    rows, cols = att.shape[1:]
    half = cols // 2
    width = raw.shape[1]
    here = pl.ds(pl.multiple_of(core * half, 128), half)
    there = pl.ds(pl.multiple_of((1 - core) * half, 128), half)
    targets = [att.at[i] for i in range(4)] + [side.at[i] for i in range(4)]
    targets += [wo.at[i, here] for i in range(4)] + [wo.at[i, there] for i in range(4)]
    copies = fetch(list(zip(sources, targets)), sem)
    for copy in copies[:4] + copies[8:]:
        copy.wait()
    raw[...] = sum(nn(att[i], wo[i]) for i in range(4))
    spots = [pl.ds(pl.multiple_of(lax.rem(head + 4 - d, 4) * cols, 128), cols) for d in DISTANCES]
    for copy in copies[4:8]:
        copy.wait()
    for i in range(4):
        raw[:, spots[i]] += side[i, :, :cols].astype(F32)
    full = raw[...]
    mean = jnp.sum(full, axis=1, keepdims=True) / width
    var = jnp.sum(full * full, axis=1, keepdims=True) / width - mean * mean
    scale = lax.rsqrt(var + EPS)
    loss = jnp.zeros((rows, 1), F32)
    for i in range(4):
        normed = (raw[:, spots[i]] - mean) * scale
        if i == 0:
            target_ref[...] = normed.astype(BF)
        gap = side[i, :, cols:].astype(F32) - normed
        loss = loss + jnp.sum(gap * gap, axis=1, keepdims=True)
    loss_ref[...] = jnp.broadcast_to(loss / width, (rows, 128)).T[:1]


def whole(n):
    return [pl.BlockSpec(memory_space=pltpu.VMEM) for _ in range(n)]


def params(mib):
    return pltpu.CompilerParams(vmem_limit_bytes=mib * 2**20)


def tm_index(z, y, c):
    return ((z % 4) * 4 + y % 4) * 2 + c


DISTANCES = (0, 1, 3, 2)
PLACES = [(z, y, c) for z in range(4) for y in range(4) for c in range(2)]
FREE = pl.BlockSpec(memory_space=pl.ANY)
HBM = pl.BlockSpec(memory_space=pltpu.HBM)


def along_y(d):
    return [(tm_index(z, y, c), tm_index(z, y + d, c)) for z, y, c in PLACES]


def along_z(d):
    return [(tm_index(z, y, c), tm_index(z + d, y, c)) for z, y, c in PLACES]


OTHER_CORE = [(t, t ^ 1) for t in range(32)]


def body(tokens, w_query, w_key, w_value, w_out, pattern, visible, slot, pred):
    n_peers = lax.axis_size("tm")
    me = lax.axis_index("tm")
    head = lax.axis_index("head")
    n_heads = lax.axis_size("head")
    frames, keep = visible.shape
    width = tokens.shape[1]
    cols = w_query.shape[1]
    own = frames * keep
    steps = frames // 4
    block = 4 * PATCHES
    chunk = 4 * keep
    padded = -(-own // 128) * 128
    my_core = me % 2

    r = np.arange(block)
    p = r % PATCHES
    quadrant = 2 * (p // 14 >= 7) + (p % 14 >= 7)
    pool = np.zeros((16, block), np.float32)
    pool[r // PATCHES * 4 + quadrant, r] = 1.0
    n = np.arange(4 * frames)
    order = np.zeros((4 * frames, 4 * frames), np.float32)
    order[n, n % frames * 4 + n // frames] = 1.0

    mine, q, tok = pl.pallas_call(
        gather_kernel,
        in_specs=[HBM] * 4 + whole(3),
        out_specs=whole(3),
        out_shape=[
            jax.ShapeDtypeStruct((4 * frames, 2 * cols), BF),
            jax.ShapeDtypeStruct((own, cols), BF),
            jax.ShapeDtypeStruct((padded, cols), BF),
        ],
        scratch_shapes=[pltpu.VMEM((frames * PATCHES, width), BF)]
        + [pltpu.VMEM((width, cols), BF)] * 3
        + [pltpu.VMEM((4 * frames, width), F32), pltpu.VMEM((own, width), BF), pltpu.SemaphoreType.DMA((steps + 3,))],
        compiler_params=params(60),
        cost_estimate=pl.CostEstimate(flops=2 * 10**9, bytes_accessed=10**7, transcendentals=0),
        name="gather",
    )(tokens, w_query, w_key, w_value, jnp.asarray(pool, BF), visible, jnp.asarray(order, BF))

    plane = jnp.stack([mine] + [lax.ppermute(mine, "tm", along_y(d)) for d in DISTANCES[1:]])
    plane, q, tok = lax.optimization_barrier((plane, q, tok))
    parts = [plane] + [lax.ppermute(plane, "tm", along_z(d)) for d in DISTANCES[1:]]
    owner_all = slot // own
    my_slots = lax.dynamic_slice_in_dim(slot, me * own, own)
    my_owner = my_slots // own
    before = np.tril(np.ones((own, own), np.float32), -1)
    same = (my_owner[:, None] == my_owner[None, :]) & (before > 0)
    place = my_owner * CAP + jnp.sum(same, axis=1, dtype=jnp.int32)
    place = jnp.pad(place, (0, padded - own), constant_values=-1)
    pack = (jnp.arange(n_peers * CAP, dtype=jnp.int32)[:, None] == place[None, :]).astype(BF)
    coming = (owner_all == me).reshape(n_peers, own)
    rank = jnp.dot(coming.astype(BF), jnp.asarray(before.T, BF), preferred_element_type=F32).astype(jnp.int32)
    rank = jnp.where(coming, rank, -1)
    hit = rank[:, None, :] == jnp.arange(CAP, dtype=jnp.int32)[None, :, None]
    student = jnp.max(jnp.where(hit, (slot % own).reshape(n_peers, 1, own), -1), axis=2)
    unpack = (jnp.arange(own, dtype=jnp.int32)[:, None] == student.reshape(1, -1)).astype(BF)

    def deliver(packed):
        return lax.all_to_all(packed, "tm", 0, 0, tiled=True)

    def arrange(got):
        return jnp.dot(unpack, got.reshape(n_peers * CAP, -1), preferred_element_type=F32).astype(BF)

    tok_got = deliver(jnp.dot(pack, tok, preferred_element_type=F32).astype(BF).reshape(n_peers, CAP, cols))

    heads = cols // HEAD_DIM
    near = pl.pallas_call(
        near_kernel,
        in_specs=[HBM] * 4,
        out_specs=pl.BlockSpec(memory_space=pltpu.VMEM),
        out_shape=jax.ShapeDtypeStruct((own * heads, cols + 128), BF),
        scratch_shapes=[pltpu.VMEM((own, cols), BF), pltpu.VMEM((frames * PATCHES, width), BF)]
        + [pltpu.VMEM((width, cols), BF)] * 2
        + [pltpu.SemaphoreType.DMA((steps + 3,))],
        compiler_params=params(60),
        cost_estimate=pl.CostEstimate(flops=5 * 10**9, bytes_accessed=10**7, transcendentals=10**6),
        name="near",
    )(q, tokens, w_key, w_value)

    plane, near = lax.optimization_barrier((plane, near))
    parts = parts + [lax.ppermute(part, "tm", OTHER_CORE) for part in [plane] + parts[1:]]
    packed = pl.pallas_call(
        far_kernel,
        in_specs=[HBM] * 13,
        out_specs=pl.BlockSpec(memory_space=pltpu.VMEM),
        out_shape=jax.ShapeDtypeStruct((n_peers, CAP, cols), BF),
        scratch_shapes=[
            pltpu.VMEM((8, 4, 4 * frames, 2 * cols), BF),
            pltpu.VMEM((4, n_peers * frames, cols), BF),
            pltpu.VMEM((4, n_peers * frames, cols), BF),
            pltpu.VMEM((own, cols), BF),
            pltpu.VMEM((own * heads, cols + 128), BF),
            pltpu.VMEM(pattern.shape, jnp.int32),
            pltpu.VMEM(pack.shape, BF),
            pltpu.SemaphoreType.DMA((12,)),
        ],
        compiler_params=params(50),
        cost_estimate=pl.CostEstimate(flops=4 * 10**9, bytes_accessed=4 * 10**6, transcendentals=3 * 10**6),
        name="far",
    )(q, near, pattern, pack, tok_got, *parts)
    tok_own = arrange(tok_got)
    packed, w_out = lax.optimization_barrier((packed, w_out))
    att = arrange(deliver(packed))

    def to(d):
        return [(h, (h + d) % n_heads) for h in range(n_heads)]

    def over_heads(x):
        return [x] + [lax.ppermute(x, "head", to(d)) for d in DISTANCES[1:]]

    half = cols // 2
    halves = over_heads(lax.dynamic_slice_in_dim(w_out, my_core * half, half, 0))
    other = [lax.ppermute(piece, "tm", OTHER_CORE) for piece in halves]
    side = over_heads(jnp.concatenate([tok_own, pred], axis=1))

    target, row_loss = pl.pallas_call(
        final_kernel,
        in_specs=[HBM] * 16,
        out_specs=whole(2),
        out_shape=[jax.ShapeDtypeStruct((own, cols), BF), jax.ShapeDtypeStruct((1, own), F32)],
        scratch_shapes=[
            pltpu.VMEM((4, own, cols), BF),
            pltpu.VMEM((4, own, 2 * cols), BF),
            pltpu.VMEM((4, cols, width), BF),
            pltpu.VMEM((own, width), F32),
            pltpu.SemaphoreType.DMA((16,)),
        ],
        compiler_params=params(16),
        cost_estimate=pl.CostEstimate(flops=10**9, bytes_accessed=4 * 10**6, transcendentals=0),
        name="final",
    )(*over_heads(att), *side, *halves, *other)
    return target, row_loss.reshape(own)


def solution(mesh):
    return jax.shard_map(
        body,
        mesh=mesh,
        in_specs=(
            P("tm", None),
            P(None, "head"),
            P(None, "head"),
            P(None, "head"),
            P("head", None),
            P("tm", None),
            P("tm", None),
            P(),
            P("tm", "head"),
        ),
        out_specs=(P("tm", "head"), P("tm")),
        check_vma=False,
    )
```

```python
import numpy as np

import jax
import jax.numpy as jnp
from jax import lax
from jax.experimental import pallas as pl
from jax.experimental.pallas import tpu as pltpu
from jax.sharding import PartitionSpec as P

HEAD_DIM = 64
PATCHES = 196
CAP = 48
NEG = -1e30
EPS = 1e-06
BF = jnp.bfloat16
F32 = jnp.float32


def nt(a, b):
    return lax.dot_general(a, b, (((1,), (1,)), ((), ())), preferred_element_type=F32)


def nn(a, b):
    return lax.dot_general(a, b, (((1,), (0,)), ((), ())), preferred_element_type=F32)


def fetch(pairs, sem):
    copies = [pltpu.make_async_copy(source, target, sem.at[i]) for i, (source, target) in enumerate(pairs)]
    for copy in copies:
        copy.start()
    return copies


def row_blocks(ref, count):
    size = ref.shape[0] // count
    return [ref.at[pl.ds(i * size, size)] for i in range(count)]


def gather_kernel(
    x_hbm, wq_hbm, wk_hbm, wv_hbm, pool_ref, vis_ref, order_ref, chunk_ref, q_ref, t_ref, x_ref, wq_ref, wk_ref, wv_ref, sums, rows_in, sem
):
    steps = vis_ref.shape[0] // 4
    pairs = list(zip(row_blocks(x_hbm, steps), row_blocks(x_ref, steps)))
    copies = fetch(pairs + [(wk_hbm, wk_ref), (wv_hbm, wv_ref), (wq_hbm, wq_ref)], sem)
    rows = x_ref.shape[0] // steps
    frames, keep = vis_ref.shape
    count = 4 * keep
    cols = wk_ref.shape[1]
    r = lax.broadcasted_iota(jnp.int32, (count, 1), 0)
    frame = sum((r >= keep * i).astype(jnp.int32) for i in (1, 2, 3))
    spot = lax.broadcasted_iota(jnp.int32, (count, keep), 1) == r - keep * frame
    for step in range(steps):
        mine = (lax.broadcasted_iota(jnp.int32, (count, frames), 1) == frame + step * 4).astype(F32).astype(BF)
        seen = nn(mine, vis_ref[...].astype(F32).astype(BF))
        pos = jnp.sum(jnp.where(spot, seen, 0.0), axis=1, keepdims=True).astype(jnp.int32) + frame * PATCHES
        pick = (pos == lax.broadcasted_iota(jnp.int32, (count, rows), 1)).astype(F32).astype(BF)
        choose = jnp.concatenate([pool_ref[...], pick], axis=0)
        copies[step].wait()
        both = nn(choose, x_ref[step * rows : (step + 1) * rows, :])
        sums[step * 16 : (step + 1) * 16, :] = both[:16]
        rows_in[step * count : (step + 1) * count, :] = both[16:].astype(BF)
    total = sums[...]
    count = total.shape[0]
    high = total.astype(BF)
    low = (total - high.astype(F32)).astype(BF)
    pair = jnp.concatenate([high, low], axis=0)
    order = order_ref[...]
    for i, w_ref in enumerate((wk_ref, wv_ref)):
        copies[steps + i].wait()
        field = nn(pair, w_ref[...])
        pooled = ((field[:count] + field[count:]) / 7.0).astype(BF)
        chunk_ref[:, i * cols : (i + 1) * cols] = nn(order, pooled).astype(BF)
    copies[steps + 2].wait()
    q = nn(rows_in[...], wq_ref[...]).astype(BF).astype(F32) * HEAD_DIM ** -0.5
    q_ref[...] = q.astype(BF)
    t_ref[q_ref.shape[0] :, :] = jnp.zeros((t_ref.shape[0] - q_ref.shape[0], cols), BF)
    t_ref[: q_ref.shape[0], :] = rows_in[:, pl.ds(pl.multiple_of(lax.axis_index("head") * cols, 128), cols)]


def row_order(keep, heads):
    rows, chunk, cols = 4 * keep * heads, 4 * keep, heads * HEAD_DIM

    def split(r):
        frame = sum((r >= keep * heads * i).astype(jnp.int32) for i in (1, 2, 3))
        r = r - frame * keep * heads
        head = sum((r >= keep * i).astype(jnp.int32) for i in range(1, heads))
        return frame * keep + r - head * keep, head

    source, head = split(lax.broadcasted_iota(jnp.int32, (rows, 1), 0))
    spread = (source == lax.broadcasted_iota(jnp.int32, (rows, chunk), 1)).astype(F32).astype(BF)
    lanes = (head == lax.broadcasted_iota(jnp.int32, (rows, cols), 1) >> 6).astype(F32).astype(BF)
    source, _ = split(lax.broadcasted_iota(jnp.int32, (1, rows), 1))
    join = (source == lax.broadcasted_iota(jnp.int32, (chunk, rows), 0)).astype(F32).astype(BF)
    return spread, lanes, join


def near_kernel(q_hbm, x_hbm, wk_hbm, wv_hbm, out_ref, q_ref, x_ref, wk_ref, wv_ref, sem):
    heads = wk_ref.shape[1] // HEAD_DIM
    steps = x_ref.shape[0] // (4 * PATCHES)
    chunk = q_ref.shape[0] // steps
    pairs = list(zip(row_blocks(x_hbm, steps), row_blocks(x_ref, steps)))
    copies = fetch([(wk_hbm, wk_ref)] + pairs[:1] + [(wv_hbm, wv_ref), (q_hbm, q_ref)] + pairs[1:], sem)
    size = x_ref.shape[0] // steps
    cols = q_ref.shape[1]
    rows = chunk // 4 * heads
    span = 208
    starts = [f * PATCHES // 16 * 16 for f in range(4)]
    c = lax.broadcasted_iota(jnp.int32, (rows, span), 1)
    walls = [jnp.where((c >= f * PATCHES - starts[f]) & (c < (f + 1) * PATCHES - starts[f]), 0.0, NEG) for f in range(4)]
    lane = lax.broadcasted_iota(jnp.int32, (4 * rows, 128), 1)
    spread, lanes, _ = row_order(chunk // 4, heads)
    for copy in copies[:4]:
        copy.wait()
    for step in range(steps):
        if step:
            copies[3 + step].wait()
        x = x_ref[step * size : (step + 1) * size, :]
        k = nn(x, wk_ref[...]).astype(BF)
        v = nn(x, wv_ref[...]).astype(BF)
        stack = nn(spread, q_ref[step * chunk : (step + 1) * chunk, :]).astype(BF) * lanes
        s = jnp.concatenate(
            [nt(stack[f * rows : (f + 1) * rows], k[starts[f] : starts[f] + span]) + walls[f] for f in range(4)], axis=0
        )
        m = jnp.max(s, axis=1, keepdims=True)
        e = jnp.exp(s - m)
        total = jnp.sum(e, axis=1, keepdims=True)
        e = e.astype(BF)
        o = jnp.concatenate(
            [nn(e[f * rows : (f + 1) * rows], v[starts[f] : starts[f] + span]) for f in range(4)], axis=0
        )
        level = m + jnp.log(total)
        high = level.astype(BF).astype(F32)
        middle = (level - high).astype(BF).astype(F32)
        side = jnp.where(lane == 0, high, jnp.where(lane == 1, middle, jnp.where(lane == 2, level - high - middle, 0.0)))
        part = slice(step * 4 * rows, (step + 1) * 4 * rows)
        out_ref[part, :cols] = (o * (1.0 / total)).astype(BF)
        out_ref[part, cols:] = side.astype(BF)


def far_kernel(q_hbm, near_hbm, allow_hbm, pack_hbm, _, *rest):
    parts, rest = rest[:8], rest[8:]
    out_ref, far_ref, key, value, q_ref, near_ref, allow_ref, pack_ref, sem = rest
    pairs = [(allow_hbm, allow_ref)] + [(part, far_ref.at[i]) for i, part in enumerate(parts)]
    copies = fetch(pairs + [(q_hbm, q_ref), (near_hbm, near_ref), (pack_hbm, pack_ref)], sem)
    cols = q_ref.shape[1]
    frames, total_frames = allow_ref.shape
    groups = frames // 4
    chunk = q_ref.shape[0] // groups
    keep = chunk // 4
    heads = cols // HEAD_DIM
    rows = chunk * heads
    spread, lanes, join = row_order(keep, heads)
    column = lax.broadcasted_iota(jnp.int32, (rows, frames), 1)
    r = lax.broadcasted_iota(jnp.int32, (rows, frames), 0)
    frame = sum((r >= keep * heads * i).astype(jnp.int32) for i in (1, 2, 3))
    me = lax.axis_index("tm")
    n = lax.broadcasted_iota(jnp.int32, (1, total_frames), 1)
    i, j = (n >> 6) & 3, (n >> 4) & 3
    z = ((me >> 3) - (i ^ (i >> 1))) & 3
    y = ((me >> 1) - (j ^ (j >> 1))) & 3
    where = ((z * 4 + y) * 2 + (me & 1 ^ (n >> 8))) * 16 + (n & 15)
    order = (lax.broadcasted_iota(jnp.int32, (total_frames, total_frames), 0) == where).astype(F32).astype(BF)
    copies[0].wait()
    wall = jnp.where(nn(allow_ref[...].astype(F32).astype(BF), order) > 0.5, 0.0, NEG).astype(BF)
    for p in range(8):
        copies[1 + p].wait()
        spot = slice(p * 64, (p + 1) * 64)
        for u in range(4):
            key[u, spot, :] = far_ref[p, :, u * 16 : (u + 1) * 16, :cols].reshape(64, cols)
            value[u, spot, :] = far_ref[p, :, u * 16 : (u + 1) * 16, cols:].reshape(64, cols)
    copies[9].wait()
    copies[10].wait()
    outs = []
    for g in range(groups):
        part = slice(g * rows, (g + 1) * rows)
        q = nn(spread, q_ref[g * chunk : (g + 1) * chunk, :]).astype(BF) * lanes
        block = nn((column == frame + 4 * g).astype(F32).astype(BF), wall)
        level = jnp.sum(near_ref[part, cols:].astype(F32), axis=1, keepdims=True)
        top = level
        scores = []
        for u in range(4):
            s = nt(q, key[u]) + block
            top = jnp.maximum(top, jnp.max(s, axis=1, keepdims=True))
            scores.append(s)
        total = jnp.exp(level - top)
        acc = total * near_ref[part, :cols].astype(F32)
        for u in range(4):
            e = jnp.exp(scores[u] - top)
            total = total + jnp.sum(e, axis=1, keepdims=True)
            acc = acc + nn(e.astype(BF), value[u])
        outs.append((acc * (1.0 / total)).astype(BF) * lanes)
    outs = [nn(join, done).astype(BF) for done in outs]
    outs.append(jnp.zeros((pack_ref.shape[1] - chunk * groups, cols), BF))
    out = jnp.concatenate(outs, axis=0)
    copies[11].wait()
    out_ref[...] = nn(pack_ref[...], out).astype(BF).reshape(out_ref.shape)


def final_kernel(*refs):
    att, side, sources, (target_ref, loss_ref, wo, raw, sem) = refs[:4], refs[4:8], refs[8:16], refs[16:]
    head, core = lax.axis_index("head"), lax.axis_index("tm") & 1
    rows, cols = att[0].shape
    half = cols // 2
    width = raw.shape[1]
    here = pl.ds(pl.multiple_of(core * half, 128), half)
    there = pl.ds(pl.multiple_of((1 - core) * half, 128), half)
    targets = [wo.at[i, here] for i in range(4)] + [wo.at[i, there] for i in range(4)]
    copies = fetch(list(zip(sources, targets)), sem)
    for copy in copies:
        copy.wait()
    raw[...] = sum(nn(att[i][...], wo[i]) for i in range(4))
    spots = [pl.ds(pl.multiple_of(lax.rem(head + 4 - d, 4) * cols, 128), cols) for d in DISTANCES]
    for i in range(4):
        raw[:, spots[i]] += side[i][:, :cols].astype(F32)
    full = raw[...]
    mean = jnp.sum(full, axis=1, keepdims=True) / width
    var = jnp.sum(full * full, axis=1, keepdims=True) / width - mean * mean
    scale = lax.rsqrt(var + EPS)
    loss = jnp.zeros((rows, 1), F32)
    for i in range(4):
        normed = (raw[:, spots[i]] - mean) * scale
        if i == 0:
            target_ref[...] = normed.astype(BF)
        gap = side[i][:, cols:].astype(F32) - normed
        loss = loss + jnp.sum(gap * gap, axis=1, keepdims=True)
    loss_ref[...] = jnp.broadcast_to(loss / width, (rows, 128)).T[0]


def whole(n):
    return [pl.BlockSpec(memory_space=pltpu.VMEM) for _ in range(n)]


def params(mib):
    return pltpu.CompilerParams(vmem_limit_bytes=mib * 2**20)


def tm_index(z, y, c):
    return ((z % 4) * 4 + y % 4) * 2 + c


DISTANCES = (0, 1, 3, 2)
PLACES = [(z, y, c) for z in range(4) for y in range(4) for c in range(2)]
FREE = pl.BlockSpec(memory_space=pl.ANY)
HBM = pl.BlockSpec(memory_space=pltpu.HBM)


def along_y(d):
    return [(tm_index(z, y, c), tm_index(z, y + d, c)) for z, y, c in PLACES]


def along_z(d):
    return [(tm_index(z, y, c), tm_index(z + d, y, c)) for z, y, c in PLACES]


OTHER_CORE = [(t, t ^ 1) for t in range(32)]


def body(tokens, w_query, w_key, w_value, w_out, pattern, visible, slot, pred):
    n_peers = lax.axis_size("tm")
    me = lax.axis_index("tm")
    head = lax.axis_index("head")
    n_heads = lax.axis_size("head")
    frames, keep = visible.shape
    width = tokens.shape[1]
    cols = w_query.shape[1]
    own = frames * keep
    steps = frames // 4
    block = 4 * PATCHES
    chunk = 4 * keep
    padded = -(-own // 128) * 128
    my_core = me % 2

    r = np.arange(block)
    p = r % PATCHES
    quadrant = 2 * (p // 14 >= 7) + (p % 14 >= 7)
    pool = np.zeros((16, block), np.float32)
    pool[r // PATCHES * 4 + quadrant, r] = 1.0
    n = np.arange(4 * frames)
    order = np.zeros((4 * frames, 4 * frames), np.float32)
    order[n, n % frames * 4 + n // frames] = 1.0

    mine, q, tok = pl.pallas_call(
        gather_kernel,
        in_specs=[HBM] * 4 + whole(3),
        out_specs=whole(3),
        out_shape=[
            jax.ShapeDtypeStruct((4 * frames, 2 * cols), BF),
            jax.ShapeDtypeStruct((own, cols), BF),
            jax.ShapeDtypeStruct((padded, cols), BF),
        ],
        scratch_shapes=[pltpu.VMEM((frames * PATCHES, width), BF)]
        + [pltpu.VMEM((width, cols), BF)] * 3
        + [pltpu.VMEM((4 * frames, width), F32), pltpu.VMEM((own, width), BF), pltpu.SemaphoreType.DMA((steps + 3,))],
        compiler_params=params(60),
        cost_estimate=pl.CostEstimate(flops=2 * 10**9, bytes_accessed=10**7, transcendentals=0),
        name="gather",
    )(tokens, w_query, w_key, w_value, jnp.asarray(pool, BF), visible, jnp.asarray(order, BF))

    plane = jnp.stack([mine] + [lax.ppermute(mine, "tm", along_y(d)) for d in DISTANCES[1:]])
    plane, q, tok = lax.optimization_barrier((plane, q, tok))
    parts = [plane] + [lax.ppermute(plane, "tm", along_z(d)) for d in DISTANCES[1:]]
    owner_all = slot // own
    my_slots = lax.dynamic_slice_in_dim(slot, me * own, own)
    my_owner = my_slots // own
    before = np.tril(np.ones((own, own), np.float32), -1)
    same = (my_owner[:, None] == my_owner[None, :]) & (before > 0)
    place = my_owner * CAP + jnp.sum(same, axis=1, dtype=jnp.int32)
    place = jnp.pad(place, (0, padded - own), constant_values=-1)
    pack = (jnp.arange(n_peers * CAP, dtype=jnp.int32)[:, None] == place[None, :]).astype(BF)
    coming = (owner_all == me).reshape(n_peers, own)
    rank = jnp.dot(coming.astype(BF), jnp.asarray(before.T, BF), preferred_element_type=F32).astype(jnp.int32)
    rank = jnp.where(coming, rank, -1)
    hit = rank[:, None, :] == jnp.arange(CAP, dtype=jnp.int32)[None, :, None]
    student = jnp.max(jnp.where(hit, (slot % own).reshape(n_peers, 1, own), -1), axis=2)
    unpack = (jnp.arange(own, dtype=jnp.int32)[:, None] == student.reshape(1, -1)).astype(BF)

    def deliver(packed):
        return lax.all_to_all(packed, "tm", 0, 0, tiled=True)

    def arrange(got):
        return jnp.dot(unpack, got.reshape(n_peers * CAP, -1), preferred_element_type=F32).astype(BF)

    tok_got = deliver(jnp.dot(pack, tok, preferred_element_type=F32).astype(BF).reshape(n_peers, CAP, cols))

    heads = cols // HEAD_DIM
    near = pl.pallas_call(
        near_kernel,
        in_specs=[HBM] * 4,
        out_specs=pl.BlockSpec(memory_space=pltpu.VMEM),
        out_shape=jax.ShapeDtypeStruct((own * heads, cols + 128), BF),
        scratch_shapes=[pltpu.VMEM((own, cols), BF), pltpu.VMEM((frames * PATCHES, width), BF)]
        + [pltpu.VMEM((width, cols), BF)] * 2
        + [pltpu.SemaphoreType.DMA((steps + 3,))],
        compiler_params=params(60),
        cost_estimate=pl.CostEstimate(flops=5 * 10**9, bytes_accessed=10**7, transcendentals=10**6),
        name="near",
    )(q, tokens, w_key, w_value)

    plane, near = lax.optimization_barrier((plane, near))
    parts = parts + [lax.ppermute(part, "tm", OTHER_CORE) for part in [plane] + parts[1:]]
    packed = pl.pallas_call(
        far_kernel,
        in_specs=[HBM] * 13,
        out_specs=pl.BlockSpec(memory_space=pltpu.VMEM),
        out_shape=jax.ShapeDtypeStruct((n_peers, CAP, cols), BF),
        scratch_shapes=[
            pltpu.VMEM((8, 4, 4 * frames, 2 * cols), BF),
            pltpu.VMEM((4, n_peers * frames, cols), BF),
            pltpu.VMEM((4, n_peers * frames, cols), BF),
            pltpu.VMEM((own, cols), BF),
            pltpu.VMEM((own * heads, cols + 128), BF),
            pltpu.VMEM(pattern.shape, jnp.int32),
            pltpu.VMEM(pack.shape, BF),
            pltpu.SemaphoreType.DMA((12,)),
        ],
        compiler_params=params(60),
        cost_estimate=pl.CostEstimate(flops=4 * 10**9, bytes_accessed=4 * 10**6, transcendentals=3 * 10**6),
        name="far",
    )(q, near, pattern, pack, tok_got[0, :16, :128], *parts)
    tok_own = arrange(tok_got)
    att = arrange(deliver(packed))

    def to(d):
        return [(h, (h + d) % n_heads) for h in range(n_heads)]

    def over_heads(x):
        return [x] + [lax.ppermute(x, "head", to(d)) for d in DISTANCES[1:]]

    half = cols // 2
    halves = over_heads(lax.dynamic_slice_in_dim(w_out, my_core * half, half, 0))
    other = [lax.ppermute(piece, "tm", OTHER_CORE) for piece in halves]
    side = over_heads(jnp.concatenate([tok_own, pred], axis=1))

    target, row_loss = pl.pallas_call(
        final_kernel,
        in_specs=whole(8) + [HBM] * 8,
        out_specs=whole(2),
        out_shape=[jax.ShapeDtypeStruct((own, cols), BF), jax.ShapeDtypeStruct((own,), F32)],
        scratch_shapes=[
            pltpu.VMEM((4, cols, width), BF),
            pltpu.VMEM((own, width), F32),
            pltpu.SemaphoreType.DMA((8,)),
        ],
        compiler_params=params(16),
        cost_estimate=pl.CostEstimate(flops=10**9, bytes_accessed=4 * 10**6, transcendentals=0),
        name="final",
    )(*over_heads(att), *side, *halves, *other)
    return target, row_loss


def solution(mesh):
    return jax.shard_map(
        body,
        mesh=mesh,
        in_specs=(
            P("tm", None),
            P(None, "head"),
            P(None, "head"),
            P(None, "head"),
            P("head", None),
            P("tm", None),
            P("tm", None),
            P(),
            P("tm", "head"),
        ),
        out_specs=(P("tm", "head"), P("tm")),
        check_vma=False,
    )
```

```python
import numpy as np

import jax
import jax.numpy as jnp
from jax import lax
from jax.experimental import pallas as pl
from jax.experimental.pallas import tpu as pltpu
from jax.sharding import PartitionSpec as P

HEAD_DIM = 64
PATCHES = 196
CAP = 48
NEG = -1e30
EPS = 1e-06
BF = jnp.bfloat16
F32 = jnp.float32


def nt(a, b):
    return lax.dot_general(a, b, (((1,), (1,)), ((), ())), preferred_element_type=F32)


def nn(a, b):
    return lax.dot_general(a, b, (((1,), (0,)), ((), ())), preferred_element_type=F32)


def fetch(pairs, sem):
    copies = [pltpu.make_async_copy(source, target, sem.at[i]) for i, (source, target) in enumerate(pairs)]
    for copy in copies:
        copy.start()
    return copies


def row_blocks(ref, count):
    size = ref.shape[0] // count
    return [ref.at[pl.ds(i * size, size)] for i in range(count)]


def gather_kernel(
    x_hbm, wq_hbm, wk_hbm, wv_hbm, pool_ref, vis_ref, order_ref, chunk_ref, q_ref, t_ref, x_ref, wq_ref, wk_ref, wv_ref, sums, rows_in, sem
):
    steps = vis_ref.shape[0] // 4
    pairs = list(zip(row_blocks(x_hbm, steps), row_blocks(x_ref, steps)))
    copies = fetch(pairs + [(wk_hbm, wk_ref), (wv_hbm, wv_ref), (wq_hbm, wq_ref)], sem)
    rows = x_ref.shape[0] // steps
    frames, keep = vis_ref.shape
    count = 4 * keep
    cols = wk_ref.shape[1]
    r = lax.broadcasted_iota(jnp.int32, (count, 1), 0)
    frame = sum((r >= keep * i).astype(jnp.int32) for i in (1, 2, 3))
    spot = lax.broadcasted_iota(jnp.int32, (count, keep), 1) == r - keep * frame
    for step in range(steps):
        mine = (lax.broadcasted_iota(jnp.int32, (count, frames), 1) == frame + step * 4).astype(F32).astype(BF)
        seen = nn(mine, vis_ref[...].astype(F32).astype(BF))
        pos = jnp.sum(jnp.where(spot, seen, 0.0), axis=1, keepdims=True).astype(jnp.int32) + frame * PATCHES
        pick = (pos == lax.broadcasted_iota(jnp.int32, (count, rows), 1)).astype(F32).astype(BF)
        choose = jnp.concatenate([pool_ref[...], pick], axis=0)
        copies[step].wait()
        both = nn(choose, x_ref[step * rows : (step + 1) * rows, :])
        sums[step * 16 : (step + 1) * 16, :] = both[:16]
        rows_in[step * count : (step + 1) * count, :] = both[16:].astype(BF)
    total = sums[...]
    count = total.shape[0]
    high = total.astype(BF)
    low = (total - high.astype(F32)).astype(BF)
    pair = jnp.concatenate([high, low], axis=0)
    order = order_ref[...]
    for i, w_ref in enumerate((wk_ref, wv_ref)):
        copies[steps + i].wait()
        field = nn(pair, w_ref[...])
        pooled = ((field[:count] + field[count:]) / 7.0).astype(BF)
        chunk_ref[:, i * cols : (i + 1) * cols] = nn(order, pooled).astype(BF)
    copies[steps + 2].wait()
    q = nn(rows_in[...], wq_ref[...]).astype(BF).astype(F32) * HEAD_DIM ** -0.5
    q_ref[...] = q.astype(BF)
    t_ref[q_ref.shape[0] :, :] = jnp.zeros((t_ref.shape[0] - q_ref.shape[0], cols), BF)
    t_ref[: q_ref.shape[0], :] = rows_in[:, pl.ds(pl.multiple_of(lax.axis_index("head") * cols, 128), cols)]


def row_order(keep, heads):
    rows, chunk, cols = 4 * keep * heads, 4 * keep, heads * HEAD_DIM

    def split(r):
        frame = sum((r >= keep * heads * i).astype(jnp.int32) for i in (1, 2, 3))
        r = r - frame * keep * heads
        head = sum((r >= keep * i).astype(jnp.int32) for i in range(1, heads))
        return frame * keep + r - head * keep, head

    source, head = split(lax.broadcasted_iota(jnp.int32, (rows, 1), 0))
    spread = (source == lax.broadcasted_iota(jnp.int32, (rows, chunk), 1)).astype(F32).astype(BF)
    lanes = (head == lax.broadcasted_iota(jnp.int32, (rows, cols), 1) >> 6).astype(F32).astype(BF)
    source, _ = split(lax.broadcasted_iota(jnp.int32, (1, rows), 1))
    join = (source == lax.broadcasted_iota(jnp.int32, (chunk, rows), 0)).astype(F32).astype(BF)
    return spread, lanes, join


def near_kernel(q_hbm, x_hbm, wk_hbm, wv_hbm, out_ref, q_ref, x_ref, wk_ref, wv_ref, sem):
    heads = wk_ref.shape[1] // HEAD_DIM
    steps = x_ref.shape[0] // (4 * PATCHES)
    chunk = q_ref.shape[0] // steps
    pairs = list(zip(row_blocks(x_hbm, steps), row_blocks(x_ref, steps)))
    copies = fetch([(wk_hbm, wk_ref)] + pairs[:1] + [(wv_hbm, wv_ref), (q_hbm, q_ref)] + pairs[1:], sem)
    size = x_ref.shape[0] // steps
    cols = q_ref.shape[1]
    rows = chunk // 4 * heads
    span = 208
    starts = [f * PATCHES // 16 * 16 for f in range(4)]
    c = lax.broadcasted_iota(jnp.int32, (rows, span), 1)
    walls = [jnp.where((c >= f * PATCHES - starts[f]) & (c < (f + 1) * PATCHES - starts[f]), 0.0, NEG) for f in range(4)]
    lane = lax.broadcasted_iota(jnp.int32, (4 * rows, 128), 1)
    spread, lanes, _ = row_order(chunk // 4, heads)
    for copy in copies[:4]:
        copy.wait()
    for step in range(steps):
        if step:
            copies[3 + step].wait()
        x = x_ref[step * size : (step + 1) * size, :]
        k = nn(x, wk_ref[...]).astype(BF)
        v = nn(x, wv_ref[...]).astype(BF)
        stack = nn(spread, q_ref[step * chunk : (step + 1) * chunk, :]).astype(BF) * lanes
        s = jnp.concatenate(
            [nt(stack[f * rows : (f + 1) * rows], k[starts[f] : starts[f] + span]) + walls[f] for f in range(4)], axis=0
        )
        m = jnp.max(s, axis=1, keepdims=True)
        e = jnp.exp(s - m)
        total = jnp.sum(e, axis=1, keepdims=True)
        e = e.astype(BF)
        o = jnp.concatenate(
            [nn(e[f * rows : (f + 1) * rows], v[starts[f] : starts[f] + span]) for f in range(4)], axis=0
        )
        level = m + jnp.log(total)
        high = level.astype(BF).astype(F32)
        middle = (level - high).astype(BF).astype(F32)
        side = jnp.where(lane == 0, high, jnp.where(lane == 1, middle, jnp.where(lane == 2, level - high - middle, 0.0)))
        part = slice(step * 4 * rows, (step + 1) * 4 * rows)
        out_ref[part, :cols] = (o * (1.0 / total)).astype(BF)
        out_ref[part, cols:] = side.astype(BF)


def far_kernel(q_hbm, near_hbm, allow_hbm, pack_hbm, *rest):
    parts, rest = rest[:8], rest[8:]
    out_ref, far_ref, key, value, q_ref, near_ref, allow_ref, pack_ref, sem = rest
    pairs = [(allow_hbm, allow_ref)] + [(part, far_ref.at[i]) for i, part in enumerate(parts)]
    copies = fetch(pairs + [(q_hbm, q_ref), (near_hbm, near_ref), (pack_hbm, pack_ref)], sem)
    cols = q_ref.shape[1]
    frames, total_frames = allow_ref.shape
    groups = frames // 4
    chunk = q_ref.shape[0] // groups
    keep = chunk // 4
    heads = cols // HEAD_DIM
    rows = chunk * heads
    spread, lanes, join = row_order(keep, heads)
    column = lax.broadcasted_iota(jnp.int32, (rows, frames), 1)
    r = lax.broadcasted_iota(jnp.int32, (rows, frames), 0)
    frame = sum((r >= keep * heads * i).astype(jnp.int32) for i in (1, 2, 3))
    me = lax.axis_index("tm")
    n = lax.broadcasted_iota(jnp.int32, (1, total_frames), 1)
    i, j = (n >> 6) & 3, (n >> 4) & 3
    z = ((me >> 3) - (i ^ (i >> 1))) & 3
    y = ((me >> 1) - (j ^ (j >> 1))) & 3
    where = ((z * 4 + y) * 2 + (me & 1 ^ (n >> 8))) * 16 + (n & 15)
    order = (lax.broadcasted_iota(jnp.int32, (total_frames, total_frames), 0) == where).astype(F32).astype(BF)
    copies[0].wait()
    wall = jnp.where(nn(allow_ref[...].astype(F32).astype(BF), order) > 0.5, 0.0, NEG).astype(BF)
    for p in range(8):
        copies[1 + p].wait()
        spot = slice(p * 64, (p + 1) * 64)
        for u in range(4):
            key[u, spot, :] = far_ref[p, :, u * 16 : (u + 1) * 16, :cols].reshape(64, cols)
            value[u, spot, :] = far_ref[p, :, u * 16 : (u + 1) * 16, cols:].reshape(64, cols)
    copies[9].wait()
    copies[10].wait()
    outs = []
    for g in range(groups):
        part = slice(g * rows, (g + 1) * rows)
        q = nn(spread, q_ref[g * chunk : (g + 1) * chunk, :]).astype(BF) * lanes
        block = nn((column == frame + 4 * g).astype(F32).astype(BF), wall)
        level = jnp.sum(near_ref[part, cols:].astype(F32), axis=1, keepdims=True)
        top = level
        scores = []
        for u in range(4):
            s = nt(q, key[u]) + block
            top = jnp.maximum(top, jnp.max(s, axis=1, keepdims=True))
            scores.append(s)
        total = jnp.exp(level - top)
        acc = total * near_ref[part, :cols].astype(F32)
        for u in range(4):
            e = jnp.exp(scores[u] - top)
            total = total + jnp.sum(e, axis=1, keepdims=True)
            acc = acc + nn(e.astype(BF), value[u])
        outs.append((acc * (1.0 / total)).astype(BF) * lanes)
    outs = [nn(join, done).astype(BF) for done in outs]
    outs.append(jnp.zeros((pack_ref.shape[1] - chunk * groups, cols), BF))
    out = jnp.concatenate(outs, axis=0)
    copies[11].wait()
    out_ref[...] = nn(pack_ref[...], out).astype(BF).reshape(out_ref.shape)


def final_kernel(*refs):
    att, side, sources, (target_ref, loss_ref, wo, raw, sem) = refs[:4], refs[4:8], refs[8:16], refs[16:]
    head, core = lax.axis_index("head"), lax.axis_index("tm") & 1
    rows, cols = att[0].shape
    half = cols // 2
    width = raw.shape[1]
    here = pl.ds(pl.multiple_of(core * half, 128), half)
    there = pl.ds(pl.multiple_of((1 - core) * half, 128), half)
    targets = [wo.at[i, here] for i in range(4)] + [wo.at[i, there] for i in range(4)]
    copies = fetch(list(zip(sources, targets)), sem)
    for copy in copies:
        copy.wait()
    raw[...] = sum(nn(att[i][...], wo[i]) for i in range(4))
    spots = [pl.ds(pl.multiple_of(lax.rem(head + 4 - d, 4) * cols, 128), cols) for d in DISTANCES]
    for i in range(4):
        raw[:, spots[i]] += side[i][:, :cols].astype(F32)
    full = raw[...]
    mean = jnp.sum(full, axis=1, keepdims=True) / width
    var = jnp.sum(full * full, axis=1, keepdims=True) / width - mean * mean
    scale = lax.rsqrt(var + EPS)
    loss = jnp.zeros((rows, 1), F32)
    for i in range(4):
        normed = (raw[:, spots[i]] - mean) * scale
        if i == 0:
            target_ref[...] = normed.astype(BF)
        gap = side[i][:, cols:].astype(F32) - normed
        loss = loss + jnp.sum(gap * gap, axis=1, keepdims=True)
    loss_ref[...] = jnp.broadcast_to(loss / width, (rows, 128)).T[0]


def whole(n):
    return [pl.BlockSpec(memory_space=pltpu.VMEM) for _ in range(n)]


def params(mib):
    return pltpu.CompilerParams(vmem_limit_bytes=mib * 2**20)


def tm_index(z, y, c):
    return ((z % 4) * 4 + y % 4) * 2 + c


DISTANCES = (0, 1, 3, 2)
PLACES = [(z, y, c) for z in range(4) for y in range(4) for c in range(2)]
FREE = pl.BlockSpec(memory_space=pl.ANY)
HBM = pl.BlockSpec(memory_space=pltpu.HBM)


def along_y(d):
    return [(tm_index(z, y, c), tm_index(z, y + d, c)) for z, y, c in PLACES]


def along_z(d):
    return [(tm_index(z, y, c), tm_index(z + d, y, c)) for z, y, c in PLACES]


OTHER_CORE = [(t, t ^ 1) for t in range(32)]


def body(tokens, w_query, w_key, w_value, w_out, pattern, visible, slot, pred):
    n_peers = lax.axis_size("tm")
    me = lax.axis_index("tm")
    head = lax.axis_index("head")
    n_heads = lax.axis_size("head")
    frames, keep = visible.shape
    width = tokens.shape[1]
    cols = w_query.shape[1]
    own = frames * keep
    steps = frames // 4
    block = 4 * PATCHES
    chunk = 4 * keep
    padded = -(-own // 128) * 128
    my_core = me % 2

    r = np.arange(block)
    p = r % PATCHES
    quadrant = 2 * (p // 14 >= 7) + (p % 14 >= 7)
    pool = np.zeros((16, block), np.float32)
    pool[r // PATCHES * 4 + quadrant, r] = 1.0
    n = np.arange(4 * frames)
    order = np.zeros((4 * frames, 4 * frames), np.float32)
    order[n, n % frames * 4 + n // frames] = 1.0

    mine, q, tok = pl.pallas_call(
        gather_kernel,
        in_specs=[HBM] * 4 + whole(3),
        out_specs=whole(3),
        out_shape=[
            jax.ShapeDtypeStruct((4 * frames, 2 * cols), BF),
            jax.ShapeDtypeStruct((own, cols), BF),
            jax.ShapeDtypeStruct((padded, cols), BF),
        ],
        scratch_shapes=[pltpu.VMEM((frames * PATCHES, width), BF)]
        + [pltpu.VMEM((width, cols), BF)] * 3
        + [pltpu.VMEM((4 * frames, width), F32), pltpu.VMEM((own, width), BF), pltpu.SemaphoreType.DMA((steps + 3,))],
        compiler_params=params(60),
        cost_estimate=pl.CostEstimate(flops=2 * 10**9, bytes_accessed=10**7, transcendentals=0),
        name="gather",
    )(tokens, w_query, w_key, w_value, jnp.asarray(pool, BF), visible, jnp.asarray(order, BF))

    plane = jnp.stack([mine] + [lax.ppermute(mine, "tm", along_y(d)) for d in DISTANCES[1:]])
    plane, q, tok = lax.optimization_barrier((plane, q, tok))
    parts = [plane] + [lax.ppermute(plane, "tm", along_z(d)) for d in DISTANCES[1:]]
    owner_all = slot // own
    my_slots = lax.dynamic_slice_in_dim(slot, me * own, own)
    my_owner = my_slots // own
    before = np.tril(np.ones((own, own), np.float32), -1)
    same = (my_owner[:, None] == my_owner[None, :]) & (before > 0)
    place = my_owner * CAP + jnp.sum(same, axis=1, dtype=jnp.int32)
    place = jnp.pad(place, (0, padded - own), constant_values=-1)
    pack = (jnp.arange(n_peers * CAP, dtype=jnp.int32)[:, None] == place[None, :]).astype(BF)
    coming = (owner_all == me).reshape(n_peers, own)
    rank = jnp.dot(coming.astype(BF), jnp.asarray(before.T, BF), preferred_element_type=F32).astype(jnp.int32)
    rank = jnp.where(coming, rank, -1)
    hit = rank[:, None, :] == jnp.arange(CAP, dtype=jnp.int32)[None, :, None]
    student = jnp.max(jnp.where(hit, (slot % own).reshape(n_peers, 1, own), -1), axis=2)
    unpack = (jnp.arange(own, dtype=jnp.int32)[:, None] == student.reshape(1, -1)).astype(BF)

    def deliver(packed):
        return lax.all_to_all(packed, "tm", 0, 0, tiled=True)

    def arrange(got):
        return jnp.dot(unpack, got.reshape(n_peers * CAP, -1), preferred_element_type=F32).astype(BF)

    tok_got = deliver(jnp.dot(pack, tok, preferred_element_type=F32).astype(BF).reshape(n_peers, CAP, cols))

    heads = cols // HEAD_DIM
    near = pl.pallas_call(
        near_kernel,
        in_specs=[HBM] * 4,
        out_specs=pl.BlockSpec(memory_space=pltpu.VMEM),
        out_shape=jax.ShapeDtypeStruct((own * heads, cols + 128), BF),
        scratch_shapes=[pltpu.VMEM((own, cols), BF), pltpu.VMEM((frames * PATCHES, width), BF)]
        + [pltpu.VMEM((width, cols), BF)] * 2
        + [pltpu.SemaphoreType.DMA((steps + 3,))],
        compiler_params=params(60),
        cost_estimate=pl.CostEstimate(flops=5 * 10**9, bytes_accessed=10**7, transcendentals=10**6),
        name="near",
    )(q, tokens, w_key, w_value)

    plane, near = lax.optimization_barrier((plane, near))
    parts = parts + [lax.ppermute(part, "tm", OTHER_CORE) for part in [plane] + parts[1:]]
    packed = pl.pallas_call(
        far_kernel,
        in_specs=[HBM] * 12,
        out_specs=pl.BlockSpec(memory_space=pltpu.VMEM),
        out_shape=jax.ShapeDtypeStruct((n_peers, CAP, cols), BF),
        scratch_shapes=[
            pltpu.VMEM((8, 4, 4 * frames, 2 * cols), BF),
            pltpu.VMEM((4, n_peers * frames, cols), BF),
            pltpu.VMEM((4, n_peers * frames, cols), BF),
            pltpu.VMEM((own, cols), BF),
            pltpu.VMEM((own * heads, cols + 128), BF),
            pltpu.VMEM(pattern.shape, jnp.int32),
            pltpu.VMEM(pack.shape, BF),
            pltpu.SemaphoreType.DMA((12,)),
        ],
        compiler_params=params(60),
        cost_estimate=pl.CostEstimate(flops=10**6, bytes_accessed=10**4, transcendentals=0),
        name="far",
    )(q, near, pattern, pack, *parts)
    packed, tok_got = lax.optimization_barrier((packed, tok_got))
    tok_own = arrange(tok_got)
    att = arrange(deliver(packed))

    def to(d):
        return [(h, (h + d) % n_heads) for h in range(n_heads)]

    def over_heads(x):
        return [x] + [lax.ppermute(x, "head", to(d)) for d in DISTANCES[1:]]

    half = cols // 2
    halves = over_heads(lax.dynamic_slice_in_dim(w_out, my_core * half, half, 0))
    other = [lax.ppermute(piece, "tm", OTHER_CORE) for piece in halves]
    side = over_heads(jnp.concatenate([tok_own, pred], axis=1))

    target, row_loss = pl.pallas_call(
        final_kernel,
        in_specs=whole(8) + [HBM] * 8,
        out_specs=whole(2),
        out_shape=[jax.ShapeDtypeStruct((own, cols), BF), jax.ShapeDtypeStruct((own,), F32)],
        scratch_shapes=[
            pltpu.VMEM((4, cols, width), BF),
            pltpu.VMEM((own, width), F32),
            pltpu.SemaphoreType.DMA((8,)),
        ],
        compiler_params=params(16),
        cost_estimate=pl.CostEstimate(flops=10**9, bytes_accessed=4 * 10**6, transcendentals=0),
        name="final",
    )(*over_heads(att), *side, *halves, *other)
    return target, row_loss


def solution(mesh):
    return jax.shard_map(
        body,
        mesh=mesh,
        in_specs=(
            P("tm", None),
            P(None, "head"),
            P(None, "head"),
            P(None, "head"),
            P("head", None),
            P("tm", None),
            P("tm", None),
            P(),
            P("tm", "head"),
        ),
        out_specs=(P("tm", "head"), P("tm")),
        check_vma=False,
    )
```

```python
import numpy as np

import jax
import jax.numpy as jnp
from jax import lax
from jax.experimental import pallas as pl
from jax.experimental.pallas import tpu as pltpu
from jax.sharding import PartitionSpec as P

HEAD_DIM = 64
PATCHES = 196
CAP = 48
NEG = -1e30
EPS = 1e-06
BF = jnp.bfloat16
F32 = jnp.float32


def nt(a, b):
    return lax.dot_general(a, b, (((1,), (1,)), ((), ())), preferred_element_type=F32)


def nn(a, b):
    return lax.dot_general(a, b, (((1,), (0,)), ((), ())), preferred_element_type=F32)


def fetch(pairs, sem):
    copies = [pltpu.make_async_copy(source, target, sem.at[i]) for i, (source, target) in enumerate(pairs)]
    for copy in copies:
        copy.start()
    return copies


def row_blocks(ref, count):
    size = ref.shape[0] // count
    return [ref.at[pl.ds(i * size, size)] for i in range(count)]


def gather_kernel(
    x_hbm, wq_hbm, wk_hbm, wv_hbm, vis_hbm, chunk_ref, q_ref, t_ref, x_ref, wq_ref, wk_ref, wv_ref, vis_ref, sums, rows_in, sem
):
    steps = vis_ref.shape[0] // 4
    pairs = list(zip(row_blocks(x_hbm, steps), row_blocks(x_ref, steps)))
    copies = fetch([(vis_hbm, vis_ref)] + pairs + [(wk_hbm, wk_ref), (wv_hbm, wv_ref), (wq_hbm, wq_ref)], sem)
    rows = x_ref.shape[0] // steps
    frames, keep = vis_ref.shape
    count = 4 * keep
    cols = wk_ref.shape[1]
    r = lax.broadcasted_iota(jnp.int32, (count, 1), 0)
    frame = sum((r >= keep * i).astype(jnp.int32) for i in (1, 2, 3))
    spot = lax.broadcasted_iota(jnp.int32, (count, keep), 1) == r - keep * frame
    c = lax.broadcasted_iota(jnp.int32, (1, rows), 1)
    f = sum((c >= PATCHES * i).astype(jnp.int32) for i in (1, 2, 3))
    p = c - f * PATCHES
    quadrant = 4 * f + 2 * (p >= 98).astype(jnp.int32) + (p - p // 14 * 14 >= 7).astype(jnp.int32)
    pool = (lax.broadcasted_iota(jnp.int32, (16, rows), 0) == quadrant).astype(F32).astype(BF)
    copies[0].wait()
    for step in range(steps):
        mine = (lax.broadcasted_iota(jnp.int32, (count, frames), 1) == frame + step * 4).astype(F32).astype(BF)
        seen = nn(mine, vis_ref[...].astype(F32).astype(BF))
        pos = jnp.sum(jnp.where(spot, seen, 0.0), axis=1, keepdims=True).astype(jnp.int32) + frame * PATCHES
        pick = (pos == lax.broadcasted_iota(jnp.int32, (count, rows), 1)).astype(F32).astype(BF)
        choose = jnp.concatenate([pool, pick], axis=0)
        copies[1 + step].wait()
        both = nn(choose, x_ref[step * rows : (step + 1) * rows, :])
        sums[step * 16 : (step + 1) * 16, :] = both[:16]
        rows_in[step * count : (step + 1) * count, :] = both[16:].astype(BF)
    total = sums[...]
    count = total.shape[0]
    high = total.astype(BF)
    low = (total - high.astype(F32)).astype(BF)
    pair = jnp.concatenate([high, low], axis=0)
    r = lax.broadcasted_iota(jnp.int32, (count, count), 0)
    source = (r - r // frames * frames) * 4 + r // frames
    order = (source == lax.broadcasted_iota(jnp.int32, (count, count), 1)).astype(F32).astype(BF)
    for i, w_ref in enumerate((wk_ref, wv_ref)):
        copies[1 + steps + i].wait()
        field = nn(pair, w_ref[...])
        pooled = ((field[:count] + field[count:]) / 7.0).astype(BF)
        chunk_ref[:, i * cols : (i + 1) * cols] = nn(order, pooled).astype(BF)
    copies[steps + 3].wait()
    q = nn(rows_in[...], wq_ref[...]).astype(BF).astype(F32) * HEAD_DIM ** -0.5
    q_ref[...] = q.astype(BF)
    t_ref[q_ref.shape[0] :, :] = jnp.zeros((t_ref.shape[0] - q_ref.shape[0], cols), BF)
    t_ref[: q_ref.shape[0], :] = rows_in[:, pl.ds(pl.multiple_of(lax.axis_index("head") * cols, 128), cols)]


def row_order(keep, heads):
    rows, chunk, cols = 4 * keep * heads, 4 * keep, heads * HEAD_DIM

    def split(r):
        frame = sum((r >= keep * heads * i).astype(jnp.int32) for i in (1, 2, 3))
        r = r - frame * keep * heads
        head = sum((r >= keep * i).astype(jnp.int32) for i in range(1, heads))
        return frame * keep + r - head * keep, head

    source, head = split(lax.broadcasted_iota(jnp.int32, (rows, 1), 0))
    spread = (source == lax.broadcasted_iota(jnp.int32, (rows, chunk), 1)).astype(F32).astype(BF)
    lanes = (head == lax.broadcasted_iota(jnp.int32, (rows, cols), 1) >> 6).astype(F32).astype(BF)
    source, _ = split(lax.broadcasted_iota(jnp.int32, (1, rows), 1))
    join = (source == lax.broadcasted_iota(jnp.int32, (chunk, rows), 0)).astype(F32).astype(BF)
    return spread, lanes, join


def near_kernel(q_hbm, x_hbm, wk_hbm, wv_hbm, out_ref, q_ref, x_ref, wk_ref, wv_ref, sem):
    heads = wk_ref.shape[1] // HEAD_DIM
    steps = x_ref.shape[0] // (4 * PATCHES)
    chunk = q_ref.shape[0] // steps
    pairs = list(zip(row_blocks(x_hbm, steps), row_blocks(x_ref, steps)))
    copies = fetch([(wk_hbm, wk_ref)] + pairs[:1] + [(wv_hbm, wv_ref), (q_hbm, q_ref)] + pairs[1:], sem)
    size = x_ref.shape[0] // steps
    cols = q_ref.shape[1]
    rows = chunk // 4 * heads
    span = 208
    starts = [f * PATCHES // 16 * 16 for f in range(4)]
    c = lax.broadcasted_iota(jnp.int32, (rows, span), 1)
    walls = [jnp.where((c >= f * PATCHES - starts[f]) & (c < (f + 1) * PATCHES - starts[f]), 0.0, NEG) for f in range(4)]
    lane = lax.broadcasted_iota(jnp.int32, (4 * rows, 128), 1)
    spread, lanes, _ = row_order(chunk // 4, heads)
    for copy in copies[:4]:
        copy.wait()
    for step in range(steps):
        if step:
            copies[3 + step].wait()
        x = x_ref[step * size : (step + 1) * size, :]
        k = nn(x, wk_ref[...]).astype(BF)
        v = nn(x, wv_ref[...]).astype(BF)
        stack = nn(spread, q_ref[step * chunk : (step + 1) * chunk, :]).astype(BF) * lanes
        s = jnp.concatenate(
            [nt(stack[f * rows : (f + 1) * rows], k[starts[f] : starts[f] + span]) + walls[f] for f in range(4)], axis=0
        )
        m = jnp.max(s, axis=1, keepdims=True)
        e = jnp.exp(s - m)
        total = jnp.sum(e, axis=1, keepdims=True)
        e = e.astype(BF)
        o = jnp.concatenate(
            [nn(e[f * rows : (f + 1) * rows], v[starts[f] : starts[f] + span]) for f in range(4)], axis=0
        )
        level = m + jnp.log(total)
        high = level.astype(BF).astype(F32)
        middle = (level - high).astype(BF).astype(F32)
        side = jnp.where(lane == 0, high, jnp.where(lane == 1, middle, jnp.where(lane == 2, level - high - middle, 0.0)))
        part = slice(step * 4 * rows, (step + 1) * 4 * rows)
        out_ref[part, :cols] = (o * (1.0 / total)).astype(BF)
        out_ref[part, cols:] = side.astype(BF)


def far_kernel(q_hbm, near_hbm, allow_hbm, pack_hbm, *rest):
    parts, rest = rest[:8], rest[8:]
    out_ref, far_ref, key, value, q_ref, near_ref, allow_ref, pack_ref, sem = rest
    pairs = [(allow_hbm, allow_ref)] + [(part, far_ref.at[i]) for i, part in enumerate(parts)]
    copies = fetch(pairs + [(q_hbm, q_ref), (near_hbm, near_ref), (pack_hbm, pack_ref)], sem)
    cols = q_ref.shape[1]
    frames, total_frames = allow_ref.shape
    groups = frames // 4
    chunk = q_ref.shape[0] // groups
    keep = chunk // 4
    heads = cols // HEAD_DIM
    rows = chunk * heads
    spread, lanes, join = row_order(keep, heads)
    column = lax.broadcasted_iota(jnp.int32, (rows, frames), 1)
    r = lax.broadcasted_iota(jnp.int32, (rows, frames), 0)
    frame = sum((r >= keep * heads * i).astype(jnp.int32) for i in (1, 2, 3))
    me = lax.axis_index("tm")
    n = lax.broadcasted_iota(jnp.int32, (1, total_frames), 1)
    i, j = (n >> 6) & 3, (n >> 4) & 3
    z = ((me >> 3) - (i ^ (i >> 1))) & 3
    y = ((me >> 1) - (j ^ (j >> 1))) & 3
    where = ((z * 4 + y) * 2 + (me & 1 ^ (n >> 8))) * 16 + (n & 15)
    order = (lax.broadcasted_iota(jnp.int32, (total_frames, total_frames), 0) == where).astype(F32).astype(BF)
    copies[0].wait()
    wall = jnp.where(nn(allow_ref[...].astype(F32).astype(BF), order) > 0.5, 0.0, NEG).astype(BF)
    for p in range(8):
        copies[1 + p].wait()
        spot = slice(p * 64, (p + 1) * 64)
        for u in range(4):
            key[u, spot, :] = far_ref[p, :, u * 16 : (u + 1) * 16, :cols].reshape(64, cols)
            value[u, spot, :] = far_ref[p, :, u * 16 : (u + 1) * 16, cols:].reshape(64, cols)
    copies[9].wait()
    copies[10].wait()
    outs = []
    for g in range(groups):
        part = slice(g * rows, (g + 1) * rows)
        q = nn(spread, q_ref[g * chunk : (g + 1) * chunk, :]).astype(BF) * lanes
        block = nn((column == frame + 4 * g).astype(F32).astype(BF), wall)
        level = jnp.sum(near_ref[part, cols:].astype(F32), axis=1, keepdims=True)
        top = level
        scores = []
        for u in range(4):
            s = nt(q, key[u]) + block
            top = jnp.maximum(top, jnp.max(s, axis=1, keepdims=True))
            scores.append(s)
        total = jnp.exp(level - top)
        acc = total * near_ref[part, :cols].astype(F32)
        for u in range(4):
            e = jnp.exp(scores[u] - top)
            total = total + jnp.sum(e, axis=1, keepdims=True)
            acc = acc + nn(e.astype(BF), value[u])
        outs.append((acc * (1.0 / total)).astype(BF) * lanes)
    outs = [nn(join, done).astype(BF) for done in outs]
    outs.append(jnp.zeros((pack_ref.shape[1] - chunk * groups, cols), BF))
    out = jnp.concatenate(outs, axis=0)
    copies[11].wait()
    out_ref[...] = nn(pack_ref[...], out).astype(BF).reshape(out_ref.shape)


def final_kernel(*refs):
    att, side, sources, (target_ref, loss_ref, wo, raw, sem) = refs[:4], refs[4:8], refs[8:16], refs[16:]
    head, core = lax.axis_index("head"), lax.axis_index("tm") & 1
    rows, cols = att[0].shape
    half = cols // 2
    width = raw.shape[1]
    here = pl.ds(pl.multiple_of(core * half, 128), half)
    there = pl.ds(pl.multiple_of((1 - core) * half, 128), half)
    targets = [wo.at[i, here] for i in range(4)] + [wo.at[i, there] for i in range(4)]
    copies = fetch(list(zip(sources, targets)), sem)
    for copy in copies:
        copy.wait()
    raw[...] = sum(nn(att[i][...], wo[i]) for i in range(4))
    spots = [pl.ds(pl.multiple_of(lax.rem(head + 4 - d, 4) * cols, 128), cols) for d in DISTANCES]
    for i in range(4):
        raw[:, spots[i]] += side[i][:, :cols].astype(F32)
    full = raw[...]
    mean = jnp.sum(full, axis=1, keepdims=True) / width
    var = jnp.sum(full * full, axis=1, keepdims=True) / width - mean * mean
    scale = lax.rsqrt(var + EPS)
    loss = jnp.zeros((rows, 1), F32)
    for i in range(4):
        normed = (raw[:, spots[i]] - mean) * scale
        if i == 0:
            target_ref[...] = normed.astype(BF)
        gap = side[i][:, cols:].astype(F32) - normed
        loss = loss + jnp.sum(gap * gap, axis=1, keepdims=True)
    loss_ref[...] = jnp.broadcast_to(loss / width, (rows, 128)).T[0]


def whole(n):
    return [pl.BlockSpec(memory_space=pltpu.VMEM) for _ in range(n)]


def params(mib):
    return pltpu.CompilerParams(vmem_limit_bytes=mib * 2**20)


def tm_index(z, y, c):
    return ((z % 4) * 4 + y % 4) * 2 + c


DISTANCES = (0, 1, 3, 2)
PLACES = [(z, y, c) for z in range(4) for y in range(4) for c in range(2)]
FREE = pl.BlockSpec(memory_space=pl.ANY)
HBM = pl.BlockSpec(memory_space=pltpu.HBM)


def along_y(d):
    return [(tm_index(z, y, c), tm_index(z, y + d, c)) for z, y, c in PLACES]


def along_z(d):
    return [(tm_index(z, y, c), tm_index(z + d, y, c)) for z, y, c in PLACES]


OTHER_CORE = [(t, t ^ 1) for t in range(32)]


def body(tokens, w_query, w_key, w_value, w_out, pattern, visible, slot, pred):
    n_peers = lax.axis_size("tm")
    me = lax.axis_index("tm")
    head = lax.axis_index("head")
    n_heads = lax.axis_size("head")
    frames, keep = visible.shape
    width = tokens.shape[1]
    cols = w_query.shape[1]
    own = frames * keep
    steps = frames // 4
    block = 4 * PATCHES
    chunk = 4 * keep
    padded = -(-own // 128) * 128
    my_core = me % 2

    mine, q, tok = pl.pallas_call(
        gather_kernel,
        in_specs=[HBM] * 5,
        out_specs=whole(3),
        out_shape=[
            jax.ShapeDtypeStruct((4 * frames, 2 * cols), BF),
            jax.ShapeDtypeStruct((own, cols), BF),
            jax.ShapeDtypeStruct((padded, cols), BF),
        ],
        scratch_shapes=[pltpu.VMEM((frames * PATCHES, width), BF)]
        + [pltpu.VMEM((width, cols), BF)] * 3
        + [pltpu.VMEM((frames, keep), jnp.int32), pltpu.VMEM((4 * frames, width), F32), pltpu.VMEM((own, width), BF)]
        + [pltpu.SemaphoreType.DMA((steps + 4,))],
        compiler_params=params(60),
        cost_estimate=pl.CostEstimate(flops=2 * 10**9, bytes_accessed=10**7, transcendentals=0),
        name="gather",
    )(tokens, w_query, w_key, w_value, visible)

    plane = jnp.stack([mine] + [lax.ppermute(mine, "tm", along_y(d)) for d in DISTANCES[1:]])
    plane, q, tok = lax.optimization_barrier((plane, q, tok))
    parts = [plane] + [lax.ppermute(plane, "tm", along_z(d)) for d in DISTANCES[1:]]
    owner_all = slot // own
    my_slots = lax.dynamic_slice_in_dim(slot, me * own, own)
    my_owner = my_slots // own
    before = np.tril(np.ones((own, own), np.float32), -1)
    same = (my_owner[:, None] == my_owner[None, :]) & (before > 0)
    place = my_owner * CAP + jnp.sum(same, axis=1, dtype=jnp.int32)
    place = jnp.pad(place, (0, padded - own), constant_values=-1)
    pack = (jnp.arange(n_peers * CAP, dtype=jnp.int32)[:, None] == place[None, :]).astype(BF)
    coming = (owner_all == me).reshape(n_peers, own)
    rank = jnp.dot(coming.astype(BF), jnp.asarray(before.T, BF), preferred_element_type=F32).astype(jnp.int32)
    rank = jnp.where(coming, rank, -1)
    hit = rank[:, None, :] == jnp.arange(CAP, dtype=jnp.int32)[None, :, None]
    student = jnp.max(jnp.where(hit, (slot % own).reshape(n_peers, 1, own), -1), axis=2)
    unpack = (jnp.arange(own, dtype=jnp.int32)[:, None] == student.reshape(1, -1)).astype(BF)

    def deliver(packed):
        return lax.all_to_all(packed, "tm", 0, 0, tiled=True)

    def arrange(got):
        return jnp.dot(unpack, got.reshape(n_peers * CAP, -1), preferred_element_type=F32).astype(BF)

    tok_got = deliver(jnp.dot(pack, tok, preferred_element_type=F32).astype(BF).reshape(n_peers, CAP, cols))

    heads = cols // HEAD_DIM
    near = pl.pallas_call(
        near_kernel,
        in_specs=[HBM] * 4,
        out_specs=pl.BlockSpec(memory_space=pltpu.VMEM),
        out_shape=jax.ShapeDtypeStruct((own * heads, cols + 128), BF),
        scratch_shapes=[pltpu.VMEM((own, cols), BF), pltpu.VMEM((frames * PATCHES, width), BF)]
        + [pltpu.VMEM((width, cols), BF)] * 2
        + [pltpu.SemaphoreType.DMA((steps + 3,))],
        compiler_params=params(60),
        cost_estimate=pl.CostEstimate(flops=5 * 10**9, bytes_accessed=10**7, transcendentals=10**6),
        name="near",
    )(q, tokens, w_key, w_value)

    plane, near = lax.optimization_barrier((plane, near))
    parts = parts + [lax.ppermute(part, "tm", OTHER_CORE) for part in [plane] + parts[1:]]
    packed = pl.pallas_call(
        far_kernel,
        in_specs=[HBM] * 12,
        out_specs=pl.BlockSpec(memory_space=pltpu.VMEM),
        out_shape=jax.ShapeDtypeStruct((n_peers, CAP, cols), BF),
        scratch_shapes=[
            pltpu.VMEM((8, 4, 4 * frames, 2 * cols), BF),
            pltpu.VMEM((4, n_peers * frames, cols), BF),
            pltpu.VMEM((4, n_peers * frames, cols), BF),
            pltpu.VMEM((own, cols), BF),
            pltpu.VMEM((own * heads, cols + 128), BF),
            pltpu.VMEM(pattern.shape, jnp.int32),
            pltpu.VMEM(pack.shape, BF),
            pltpu.SemaphoreType.DMA((12,)),
        ],
        compiler_params=params(60),
        cost_estimate=pl.CostEstimate(flops=10**6, bytes_accessed=10**4, transcendentals=0),
        name="far",
    )(q, near, pattern, pack, *parts)
    packed, tok_got = lax.optimization_barrier((packed, tok_got))
    tok_own = arrange(tok_got)
    att = arrange(deliver(packed))

    def to(d):
        return [(h, (h + d) % n_heads) for h in range(n_heads)]

    def over_heads(x):
        return [x] + [lax.ppermute(x, "head", to(d)) for d in DISTANCES[1:]]

    half = cols // 2
    halves = over_heads(lax.dynamic_slice_in_dim(w_out, my_core * half, half, 0))
    other = [lax.ppermute(piece, "tm", OTHER_CORE) for piece in halves]
    side = over_heads(jnp.concatenate([tok_own, pred], axis=1))

    target, row_loss = pl.pallas_call(
        final_kernel,
        in_specs=whole(8) + [HBM] * 8,
        out_specs=whole(2),
        out_shape=[jax.ShapeDtypeStruct((own, cols), BF), jax.ShapeDtypeStruct((own,), F32)],
        scratch_shapes=[
            pltpu.VMEM((4, cols, width), BF),
            pltpu.VMEM((own, width), F32),
            pltpu.SemaphoreType.DMA((8,)),
        ],
        compiler_params=params(16),
        cost_estimate=pl.CostEstimate(flops=10**9, bytes_accessed=4 * 10**6, transcendentals=0),
        name="final",
    )(*over_heads(att), *side, *halves, *other)
    return target, row_loss


def solution(mesh):
    return jax.shard_map(
        body,
        mesh=mesh,
        in_specs=(
            P("tm", None),
            P(None, "head"),
            P(None, "head"),
            P(None, "head"),
            P("head", None),
            P("tm", None),
            P("tm", None),
            P(),
            P("tm", "head"),
        ),
        out_specs=(P("tm", "head"), P("tm")),
        check_vma=False,
    )
```
